32 devices in a mesh: ctx: 8 (over z, core), head: 4 (over y, x).
Axes of the slice: x: 2, y: 2, z: 4, core: 2. Of those that a mesh axis runs over, the one named last changes fastest.
Arguments:
- tokens: bfloat16 [2048, 2048], P('ctx'), may hold values from -15 to 15
- w_qkv: bfloat16 [3, 2048, 2048], P(None, None, 'head'), may hold values from -0.9943689 to 0.9943689
- w_out: bfloat16 [2048, 2048], P('head'), may hold values from -0.125 to 0.125
- w_dec: bfloat16 [2048, 12, 256], P(None, None, 'head'), may hold values from -0.125 to 0.125
Outputs:
- field: float32 [2048, 8, 256], P('ctx', None, 'head')
The draws below stay inside these ranges and needn't reach their ends.
All inputs are finite; a program needn't handle non-finite values.
Results may differ from the reference program's by a relative error of at most 0.011.
Values may be sent and summed in bfloat16 or wider, within the bound.
No kernel may reach another device: no remote copies, remote signals or barrier semaphores. Data moves between devices by JAX's collectives and lax.ppermute only.
A program may use at most 64 MiB of HBM per device.

```python
import math
import jax
import jax.numpy as jnp
from jax import lax

D = 2048
HEADS = 32
HD = 64
PATCH = 8
OV = 2
TOK_DEV = 256
TOKENS = 2048
XE = 12
CELLS = 256


def draw_tokens(key, part):
    first = jax.random.fold_in(key, 11)
    second = jax.random.fold_in(key, 12)
    columns = jnp.exp(jax.random.uniform(second, (D,), jnp.float32) * math.log(10.0)) / 4.0
    values = jnp.clip(jax.random.normal(first, (TOKENS, D), jnp.float32), -6.0, 6.0) * columns[None, :]
    return values.astype(jnp.bfloat16)


def draw_w_qkv(key, part):
    first = jax.random.fold_in(key, 21)
    width = HEADS * HD
    base = jnp.clip(jax.random.normal(first, (3, D, width), jnp.float32), -6.0, 6.0) * D ** (-0.5)
    stacked = base * jnp.array([3.0, 1.0, 1.0], jnp.float32).reshape(3, 1, 1)
    return stacked.astype(jnp.bfloat16)


def shard_levels(stream_key, extent, shards, least, high):
    factor_of = 1.0
    for dim, parts in shards:
        draws = jax.random.uniform(jax.random.fold_in(jax.random.fold_in(stream_key, 6), dim), (parts,), jnp.float32, least / len(shards), high / len(shards))
        factor_of = factor_of * jnp.repeat(jnp.exp(draws), extent[dim] // parts).reshape((-1,) + (1,) * (len(extent) - 1 - dim))
    return factor_of


def gaussian(key, shape, scale, bound, shards=(), held_as=jnp.bfloat16):
    entries = jax.random.normal(key, shape, jnp.float32) * scale
    if len(shards) > 0:
        entries = shard_levels(key, shape, shards, -0.22, 0.18) * entries
    return jnp.clip(entries, min=-bound, max=bound).astype(held_as)


def setup_inputs(seed: int = 0) -> dict:
    seeds = jax.random.split(jax.random.key(seed), 5)
    return {
        "tokens": draw_tokens(jax.random.fold_in(seeds[4], 71), 0),
        "w_qkv": draw_w_qkv(jax.random.fold_in(seeds[4], 71), 0),
        "w_out": gaussian(seeds[2], (HEADS * HD, D), (HEADS * HD) ** -0.5, 0.125, ((0, 4),)),
        "w_dec": gaussian(seeds[3], (D, XE, CELLS), D ** -0.5, 0.125, ((2, 4),)),
    }


def rms_scale(values):
    return values * lax.rsqrt(lax.optimization_barrier(jnp.mean(values * values, axis=-1, keepdims=True)) + 1e-05)

def reference(tokens, w_qkv, w_out, w_dec):
    xf = tokens.astype(jnp.float32)
    normed = rms_scale(xf).astype(jnp.bfloat16)
    projected = jnp.einsum('td,kdc->ktc', normed.astype(jnp.float32), w_qkv.astype(jnp.float32)).astype(jnp.bfloat16)
    queries = projected[0].reshape(TOKENS, HEADS, HD).transpose(1, 0, 2)
    keys = projected[1].reshape(TOKENS, HEADS, HD).transpose(1, 0, 2)
    values = projected[2].reshape(TOKENS, HEADS, HD).transpose(1, 0, 2)
    span = math.gcd(TOKENS, 1024)
    scale = HD ** (-0.5)

    def one_head(items):
        head_q, head_k, head_v = items

        def one_block(block_q):
            scores = jnp.dot(block_q, head_k.T, preferred_element_type=jnp.float32) * scale
            top = lax.optimization_barrier(jnp.max(scores, axis=-1, keepdims=True))
            weights = jnp.exp(scores - top)
            total = lax.optimization_barrier(jnp.sum(weights, axis=-1, keepdims=True))
            summed = jnp.dot(weights.astype(jnp.bfloat16), head_v, preferred_element_type=jnp.float32)
            return summed / total
        return lax.map(one_block, head_q.reshape(TOKENS // span, span, HD)).reshape(TOKENS, HD)
    attended = lax.map(one_head, (queries, keys, values))
    attended = attended.transpose(1, 0, 2).reshape(TOKENS, HEADS * HD).astype(jnp.bfloat16)
    mixed = jnp.dot(attended, w_out, preferred_element_type=jnp.float32)
    hidden = rms_scale(xf + mixed).astype(jnp.bfloat16)
    extended = jnp.dot(hidden, w_dec.reshape(D, XE * CELLS), preferred_element_type=jnp.float32).reshape(TOKENS, XE, CELLS)
    before = jnp.roll(extended, TOK_DEV, axis=0)
    after = jnp.roll(extended, -TOK_DEV, axis=0)
    field = jnp.concatenate([extended[:, OV:2 * OV] + before[:, PATCH + OV:], extended[:, 2 * OV:PATCH], extended[:, PATCH:PATCH + OV] + after[:, :OV]], axis=1)
    return field
```

```python
import functools
import math

import jax
import jax.numpy as jnp
from jax import lax
from jax.experimental import pallas as pl
from jax.experimental.pallas import tpu as pltpu
from jax.sharding import PartitionSpec as P

HD = 64
PATCH = 8
OV = 2
LANES = 128

eps = 1e-05
bf16 = jnp.bfloat16
f32 = jnp.float32


def passed_along(value, axis, steps):
    count = lax.axis_size(axis)
    pairs = [(source, (source + steps) % count) for source in range(count)]
    return lax.ppermute(value, axis, pairs)


def swapped(value, axis, bits):
    count = lax.axis_size(axis)
    return lax.ppermute(value, axis, [(i, i ^ bits) for i in range(count)])


def rms_scale(values):
    return values * lax.rsqrt(jnp.mean(values * values, axis=-1, keepdims=True) + eps)


def qkv_kernel(pos, x_ref, w_ref, kva, kvb, qa, qb, scale_ref):
    step = pl.program_id(0)

    @pl.when(step == 0)
    def _():
        x = x_ref[...].astype(f32)
        scale_ref[...] = lax.rsqrt(jnp.mean(x * x, axis=-1, keepdims=True) + eps)

    out = jnp.dot(x_ref[...], w_ref[0], preferred_element_type=f32) * scale_ref[...]
    odd = pos[1]

    @pl.when(step < 2)
    def _():
        kv = out.astype(bf16)

        @pl.when(odd == 0)
        def _():
            kva[step] = kv[:, :LANES]
            kvb[step] = kv[:, LANES:]

        @pl.when(odd == 1)
        def _():
            kvb[step] = kv[:, :LANES]
            kva[step] = kv[:, LANES:]

    @pl.when(step == 2)
    def _():
        q = (out * (HD ** (-0.5) * math.log2(math.e))).astype(bf16)

        @pl.when(odd == 0)
        def _():
            qa[...] = q[:, :LANES]
            qb[...] = q[:, LANES:]

        @pl.when(odd == 1)
        def _():
            qb[...] = q[:, :LANES]
            qa[...] = q[:, LANES:]


def project(pos, tokens, w_qkv):
    rows, width = tokens.shape
    whole2 = lambda i, pos: (0, 0)
    whole3 = lambda i, pos: (0, 0, 0)
    kv = jax.ShapeDtypeStruct((2, rows, LANES), bf16)
    q = jax.ShapeDtypeStruct((rows, LANES), bf16)
    return pl.pallas_call(
        qkv_kernel,
        grid_spec=pltpu.PrefetchScalarGridSpec(
            num_scalar_prefetch=1,
            grid=(3,),
            in_specs=[
                pl.BlockSpec((rows, width), whole2),
                pl.BlockSpec((1, width, 2 * LANES), lambda i, pos: (lax.rem(i + 1, 3), 0, pos[0])),
            ],
            out_specs=[
                pl.BlockSpec((2, rows, LANES), whole3),
                pl.BlockSpec((2, rows, LANES), whole3),
                pl.BlockSpec((rows, LANES), whole2),
                pl.BlockSpec((rows, LANES), whole2),
            ],
            scratch_shapes=[pltpu.VMEM((rows, 1), f32)],
        ),
        out_shape=[kv, kv, q, q],
        compiler_params=pltpu.CompilerParams(vmem_limit_bytes=24 * 2**20),
        name="project",
    )(pos, tokens, w_qkv)


def attention_kernel(tile, *refs):
    qs, kvs, outs = refs[:4], refs[4:12], refs[12:16]
    k_all, v_lo, v_hi = refs[16:19]
    rows = qs[0].shape[0]
    low = lax.broadcasted_iota(jnp.int32, (1, LANES), 1) < HD
    one = jnp.ones((), bf16)
    zero = jnp.zeros((), bf16)
    for i, kv in enumerate(kvs):
        part = pl.ds(i * rows, rows)
        k_all[part] = kv[0]
        v = kv[1]
        v_lo[part] = jnp.where(low, v, one)
        v_hi[part] = jnp.where(low, one, v)

    def weigh(q, v_ref):
        scores = lax.dot_general(q, k_all[...], (((1,), (1,)), ((), ())), preferred_element_type=f32)
        top = jnp.max(scores, axis=-1, keepdims=True)
        weights = jnp.exp2(scores - top).astype(bf16)
        return jnp.dot(weights, v_ref[...], preferred_element_type=f32)

    for q_ref, o_ref in zip(qs, outs):

        def one_tile(t, carry):
            part = pl.ds(pl.multiple_of(t * tile, tile), tile)
            q = q_ref[part]
            lo = weigh(jnp.where(low, q, zero), v_lo)
            hi = weigh(jnp.where(low, zero, q), v_hi)
            top = jnp.where(low, lo, hi)
            bottom = pltpu.roll(jnp.where(low, hi, lo), HD, 1)
            o_ref[part] = (top / bottom).astype(bf16)
            return carry

        lax.fori_loop(0, rows // tile, one_tile, 0)


def attend(qs, kvs):
    rows = qs[0].shape[0]
    keys = rows * len(kvs)
    vmem = pl.BlockSpec(memory_space=pltpu.VMEM)
    return pl.pallas_call(
        functools.partial(attention_kernel, 128),
        in_specs=[vmem] * (len(qs) + len(kvs)),
        out_specs=[vmem] * len(qs),
        out_shape=[jax.ShapeDtypeStruct(q.shape, bf16) for q in qs],
        scratch_shapes=[pltpu.VMEM((keys, LANES), bf16)] * 3,
        compiler_params=pltpu.CompilerParams(vmem_limit_bytes=32 * 2**20),
        name="attend",
    )(*qs, *kvs)


def decode_kernel(pos, x_ref, dec_ref, *refs):
    atts = refs[:16]
    own = refs[16]
    near, far = refs[17:23], refs[23:29]
    main, up, down = refs[29:32]
    att, total = refs[32:34]
    z, core = pos[0], pos[1]
    half = own.shape[0] // 2
    quarter = half // 2
    total[...] = x_ref[...].astype(f32)
    for r in range(4):
        for s in range(4):
            at = pl.multiple_of((z ^ s) * LANES, LANES)
            att[r, :, pl.ds(at, LANES)] = atts[4 * r + s][...]
    total[...] += jnp.dot(att[0], own[...], preferred_element_type=f32)
    for r in range(1, 4):
        for group, side in ((near, core), (far, 1 - core)):
            w = jnp.concatenate([group[2 * (r - 1)][...], group[2 * (r - 1) + 1][...]], axis=0)
            at = pl.multiple_of(side * half, half)
            total[...] += jnp.dot(att[r, :, pl.ds(at, half)], w, preferred_element_type=f32)
    hidden = rms_scale(total[...]).astype(bf16)
    ext = lax.dot_general(
        dec_ref[...], hidden, (((1,), (1,)), ((), ())), preferred_element_type=f32
    )
    cells = main.shape[0] // PATCH
    main[...] = ext[OV * cells : (OV + PATCH) * cells]
    down[...] = ext[: OV * cells].astype(bf16)
    up[...] = ext[(OV + PATCH) * cells :].astype(bf16)


def decode(pos, tokens, w_dec, atts, own, near, far):
    rows, width = tokens.shape
    wide = w_dec.shape[0]
    cells = wide // (PATCH + 2 * OV)
    vmem = pl.BlockSpec(memory_space=pltpu.VMEM)
    return pl.pallas_call(
        decode_kernel,
        in_specs=[pl.BlockSpec(memory_space=pltpu.SMEM)] + [vmem] * (3 + 16 + 12),
        out_specs=[vmem] * 3,
        out_shape=[
            jax.ShapeDtypeStruct((PATCH * cells, rows), f32),
            jax.ShapeDtypeStruct((OV * cells, rows), bf16),
            jax.ShapeDtypeStruct((OV * cells, rows), bf16),
        ],
        scratch_shapes=[pltpu.VMEM((4, rows, width // 4), bf16), pltpu.VMEM((rows, width), f32)],
        compiler_params=pltpu.CompilerParams(vmem_limit_bytes=40 * 2**20),
        name="decode",
    )(pos, tokens, w_dec, *atts, own, *near, *far)


def fast_body(tokens, w_qkv, w_out, w_dec):
    rows = tokens.shape[0]
    ctx = lax.axis_index("ctx")
    z, core = ctx // 2, ctx % 2
    far_pos = jnp.stack([(z // 2) ^ 1, z % 2])
    near_pos = jnp.stack([z // 2, z % 2])

    half = w_out.shape[0] // 2
    quarter = half // 2
    mine = lax.dynamic_slice_in_dim(w_out, core * half, half, 0)
    first, second = mine[:quarter], mine[quarter:]
    x_first, y_second = swapped(first, "head", 1), swapped(second, "head", 2)

    kv2, kv3, q2, q3 = project(far_pos, tokens, w_qkv)
    kv2r, kv3r = swapped(kv2, "ctx", 4), swapped(kv3, "ctx", 6)
    kv0, kv1, q0, q1 = project(near_pos, tokens, w_qkv)
    kv1r = swapped(kv1, "ctx", 2)
    q2r, q3r, q1r = swapped(q2, "ctx", 4), swapped(q3, "ctx", 6), swapped(q1, "ctx", 2)

    x_second, y_first = swapped(second, "head", 1), swapped(first, "head", 2)
    diag_first, diag_second = swapped(x_first, "head", 2), swapped(y_second, "head", 1)
    near = [x_first, x_second, y_first, y_second, diag_first, diag_second]
    far = [swapped(part, "ctx", 1) for part in near]

    kvs = [kv0, kv1r, kv2r, kv3r]
    kvs = kvs + [swapped(kv, "ctx", 1) for kv in kvs]
    o0, o1, o2, o3 = attend([q0, q1r, q2r, q3r], kvs)
    att0 = [o0, swapped(o1, "ctx", 2), swapped(o2, "ctx", 4), swapped(o3, "ctx", 6)]
    att1 = [swapped(part, "head", 1) for part in att0]
    att2 = [swapped(part, "head", 2) for part in att0]
    att3 = [swapped(att1[s], "head", 2) if s < 2 else swapped(att2[s], "head", 1) for s in range(4)]

    dec = w_dec.transpose(1, 2, 0)
    dec = dec.reshape(-1, dec.shape[2])
    main, up, down = decode(
        jnp.stack([z, core]), tokens, dec, att0 + att1 + att2 + att3, w_out, near, far
    )
    from_before = passed_along(up, "ctx", 1).astype(f32)
    from_after = passed_along(down, "ctx", -1).astype(f32)
    edge = up.shape[0]
    field = jnp.concatenate(
        [main[:edge] + from_before, main[edge:-edge], main[-edge:] + from_after], axis=0
    )
    return field.reshape(PATCH, -1, rows).transpose(2, 0, 1)


def general_body(tokens, w_qkv, w_out, w_dec):
    rows = tokens.shape[0]
    local_heads = w_qkv.shape[2] // HD
    xf = tokens.astype(f32)
    normed = rms_scale(xf).astype(bf16)
    projected = jnp.einsum("td,kdc->ktc", normed, w_qkv, preferred_element_type=f32).astype(bf16)
    queries = projected[0].reshape(rows, local_heads, HD)
    keyvals = projected[1:]
    scale = HD ** (-0.5)

    def block_update(carry, block):
        best, total, accum = carry
        keys = block[0].reshape(-1, local_heads, HD)
        values = block[1].reshape(-1, local_heads, HD)
        scores = jnp.einsum("thd,rhd->thr", queries, keys, preferred_element_type=f32) * scale
        fresh = jnp.maximum(best, jnp.max(scores, axis=-1))
        shrink = jnp.exp(best - fresh)
        weights = jnp.exp(scores - fresh[..., None])
        total = total * shrink + jnp.sum(weights, axis=-1)
        accum = accum * shrink[..., None] + jnp.einsum(
            "thr,rhd->thd", weights.astype(bf16), values, preferred_element_type=f32
        )
        return (fresh, total, accum)

    initial = (
        jnp.full((rows, local_heads), -1e30, f32),
        jnp.zeros((rows, local_heads), f32),
        jnp.zeros((rows, local_heads, HD), f32),
    )
    piece = lax.all_gather(keyvals, "ctx", axis=1, tiled=True)
    length = piece.shape[1]
    span = math.gcd(length, 1024)

    def one_block(index, inner):
        block = lax.dynamic_slice_in_dim(piece, index * span, span, 1)
        return block_update(inner, block)

    best, total, accum = lax.fori_loop(0, length // span, one_block, initial)
    attended = (accum / total[..., None]).astype(bf16).reshape(rows, local_heads * HD)
    partial_out = jnp.dot(attended, w_out, preferred_element_type=f32)
    mixed = lax.psum(partial_out.astype(bf16), "head").astype(f32)
    hidden = rms_scale(xf + mixed).astype(bf16)
    extended = jnp.dot(hidden, w_dec.reshape(w_dec.shape[0], -1), preferred_element_type=f32)
    extended = extended.reshape(rows, w_dec.shape[1], w_dec.shape[2])
    from_before = passed_along(extended[:, PATCH + OV :].astype(bf16), "ctx", 1).astype(f32)
    from_after = passed_along(extended[:, :OV].astype(bf16), "ctx", -1).astype(f32)
    middle = extended[:, OV : OV + PATCH]
    return jnp.concatenate(
        [
            middle[:, :OV] + from_before,
            middle[:, OV : PATCH - OV],
            middle[:, PATCH - OV :] + from_after,
        ],
        axis=1,
    )


def body(tokens, w_qkv, w_out, w_dec):
    fits = lax.axis_size("ctx") == 8 and lax.axis_size("head") == 4
    fits = fits and w_qkv.shape[2] == 4 * LANES and tokens.shape[0] % 256 == 0
    run = fast_body if fits else general_body
    return run(tokens, w_qkv, w_out, w_dec)


def solution(mesh):
    return jax.shard_map(
        body,
        mesh=mesh,
        in_specs=(P("ctx", None), P(None, None, "head"), P("head", None), P(None, None, "head")),
        out_specs=P("ctx", None, "head"),
        check_vma=False,
    )
```

```python
import functools
import math

import jax
import jax.numpy as jnp
from jax import lax
from jax.experimental import pallas as pl
from jax.experimental.pallas import tpu as pltpu
from jax.sharding import PartitionSpec as P

HD = 64
PATCH = 8
OV = 2
LANES = 128

eps = 1e-05
bf16 = jnp.bfloat16
f32 = jnp.float32


def passed_along(value, axis, steps):
    count = lax.axis_size(axis)
    pairs = [(source, (source + steps) % count) for source in range(count)]
    return lax.ppermute(value, axis, pairs)


def swapped(value, axis, bits):
    count = lax.axis_size(axis)
    return lax.ppermute(value, axis, [(i, i ^ bits) for i in range(count)])


def rms_scale(values):
    return values * lax.rsqrt(jnp.mean(values * values, axis=-1, keepdims=True) + eps)


def project_kernel(pos, x_hbm, w_hbm, out_hbm, *refs):
    packs, half_hbm = refs[:4], refs[4]
    x_ref, w_ref, x_sem, w_sem, half_sem = refs[5:]
    z, core = pos[0], pos[1]
    rows = x_ref.shape[0]
    pairs = [(z // 2) ^ 1, z // 2]
    copies = []
    for i, pair in enumerate(pairs):
        for k in range(3):
            cols = pl.ds(pl.multiple_of(pair * 2 * LANES, 2 * LANES), 2 * LANES)
            n = 3 * i + k
            copies.append(pltpu.make_async_copy(w_hbm.at[k, :, cols], w_ref.at[n], w_sem.at[n]))
    x_copy = pltpu.make_async_copy(x_hbm, x_ref, x_sem)
    x_copy.start()
    for copy in copies:
        copy.start()
    half = half_hbm.shape[0]
    half_copy = pltpu.make_async_copy(
        out_hbm.at[pl.ds(pl.multiple_of(core * half, half), half)], half_hbm, half_sem
    )
    half_copy.start()
    x_copy.wait()
    x = x_ref[...].astype(f32)
    scale = lax.rsqrt(jnp.mean(x * x, axis=-1, keepdims=True) + eps)
    q_scale = scale * (HD ** (-0.5) * math.log2(math.e))
    odd = z % 2
    for i in range(2):
        even_pack, odd_pack = packs[2 * (1 - i)], packs[2 * (1 - i) + 1]
        for k in range(3):
            copies[3 * i + k].wait()
            out = jnp.dot(x_ref[...], w_ref[3 * i + k], preferred_element_type=f32)
            out = (out * (q_scale if k == 0 else scale)).astype(bf16)
            left, right = out[:, :LANES], out[:, LANES:]
            part = pl.ds(k * rows, rows)
            even_pack[part] = jnp.where(odd == 0, left, right)
            odd_pack[part] = jnp.where(odd == 0, right, left)
    half_copy.wait()


def project(pos, tokens, w_qkv, w_out):
    rows, width = tokens.shape
    hbm = pl.BlockSpec(memory_space=pltpu.HBM)
    vmem = pl.BlockSpec(memory_space=pltpu.VMEM)
    pack = jax.ShapeDtypeStruct((3 * rows, LANES), bf16)
    return pl.pallas_call(
        project_kernel,
        in_specs=[pl.BlockSpec(memory_space=pltpu.SMEM), hbm, hbm, hbm],
        out_specs=[vmem] * 4 + [hbm],
        out_shape=[pack] * 4 + [jax.ShapeDtypeStruct((w_out.shape[0] // 2, width), bf16)],
        scratch_shapes=[
            pltpu.VMEM((rows, width), bf16),
            pltpu.VMEM((6, width, 2 * LANES), bf16),
            pltpu.SemaphoreType.DMA(()),
            pltpu.SemaphoreType.DMA((6,)),
            pltpu.SemaphoreType.DMA(()),
        ],
        compiler_params=pltpu.CompilerParams(vmem_limit_bytes=60 * 2**20),
        name="project",
    )(pos, tokens, w_qkv, w_out)


def attention_kernel(*refs):
    packs, outs = refs[:8], refs[8:10]
    k_all, v_lo, v_hi, q_all = refs[10:]
    rows = packs[0].shape[0] // 3
    low = lax.broadcasted_iota(jnp.int32, (1, LANES), 1) < HD
    one = jnp.ones((), bf16)
    zero = jnp.zeros((), bf16)
    for i, pack in enumerate(packs):
        part = pl.ds(i * rows, rows)
        k_all[part] = pack[rows : 2 * rows]
        v = pack[2 * rows :]
        v_lo[part] = jnp.where(low, v, one)
        v_hi[part] = jnp.where(low, one, v)
    for i in range(2):
        q_all[pl.ds(i * rows, rows)] = packs[i][:rows]

    def score(q):
        return lax.dot_general(
            q, k_all[...], (((1,), (1,)), ((), ())), preferred_element_type=f32
        )

    def weigh(scores):
        return jnp.exp2(scores - jnp.max(scores, axis=-1, keepdims=True)).astype(bf16)

    q = q_all[...]
    lo_scores = score(jnp.where(low, q, zero))
    hi_scores = score(jnp.where(low, zero, q))
    lo_weights, hi_weights = weigh(lo_scores), weigh(hi_scores)
    lo = jnp.dot(lo_weights, v_lo[...], preferred_element_type=f32)
    hi = jnp.dot(hi_weights, v_hi[...], preferred_element_type=f32)
    top = jnp.where(low, lo, hi)
    bottom = pltpu.roll(jnp.where(low, hi, lo), HD, 1)
    attended = (top / bottom).astype(bf16)
    for i in range(2):
        outs[i][...] = attended[i * rows : (i + 1) * rows]


def attend(packs):
    rows = packs[0].shape[0] // 3
    keys = rows * len(packs)
    vmem = pl.BlockSpec(memory_space=pltpu.VMEM)
    return pl.pallas_call(
        attention_kernel,
        in_specs=[vmem] * len(packs),
        out_specs=[vmem] * 2,
        out_shape=[jax.ShapeDtypeStruct((rows, LANES), bf16)] * 2,
        scratch_shapes=[pltpu.VMEM((keys, LANES), bf16)] * 3 + [pltpu.VMEM((2 * rows, LANES), bf16)],
        compiler_params=pltpu.CompilerParams(vmem_limit_bytes=24 * 2**20),
        name="attend",
    )(*packs)


def mix_kernel(pos, x_ref, o0, o1, o2, own, n1, f2, n2, f1, total, att):
    z, core = pos[0], pos[1]
    rows, width = x_ref.shape
    local = own.shape[0]
    for s in range(4):
        place = z ^ s
        part = pl.ds(s * rows, rows)
        att[:, pl.ds(pl.multiple_of(place * LANES, LANES), LANES)] = o0[part]
        place = place ^ (2 * core)
        for i, o in enumerate((o1, o2)):
            at = pl.multiple_of((i + 1) * local + place * LANES, LANES)
            att[:, pl.ds(at, LANES)] = o[part]
    step = 512
    for n in range(0, width, step):
        w = jnp.concatenate([part[:, n : n + step] for part in (own, n1, f2, n2, f1)], axis=0)
        mixed = jnp.dot(att[...], w, preferred_element_type=f32)
        total[:, n : n + step] = x_ref[:, n : n + step].astype(f32) + mixed


def mix(pos, tokens, outs, parts):
    rows, width = tokens.shape
    vmem = pl.BlockSpec(memory_space=pltpu.VMEM)
    return pl.pallas_call(
        mix_kernel,
        in_specs=[pl.BlockSpec(memory_space=pltpu.SMEM)] + [vmem] * 9,
        out_specs=vmem,
        out_shape=jax.ShapeDtypeStruct((rows, width), f32),
        scratch_shapes=[pltpu.VMEM((rows, 3 * parts[0].shape[0]), bf16)],
        compiler_params=pltpu.CompilerParams(vmem_limit_bytes=12 * 2**20),
        name="mix",
    )(pos, tokens, *outs, *parts)


def decode_kernel(pos, total, o3, n3, f3, dec_ref, main, up, down, att, hidden):
    z, core = pos[0], pos[1]
    rows, width = total.shape
    for s in range(4):
        place = z ^ s ^ (2 * core)
        att[:, pl.ds(pl.multiple_of(place * LANES, LANES), LANES)] = o3[pl.ds(s * rows, rows)]
    step = 512
    squares = jnp.zeros((rows, LANES), f32)
    for n in range(0, width, step):
        w = jnp.concatenate([part[:, n : n + step] for part in (n3, f3)], axis=0)
        mixed = total[:, n : n + step] + jnp.dot(att[...], w, preferred_element_type=f32)
        hidden[:, n : n + step] = mixed
        for i in range(0, step, LANES):
            squares += mixed[:, i : i + LANES] * mixed[:, i : i + LANES]
    scale = lax.rsqrt(jnp.sum(squares, axis=-1, keepdims=True) * (1.0 / width) + eps)
    ext = lax.dot_general(
        dec_ref[...],
        (hidden[...] * scale).astype(bf16),
        (((1,), (1,)), ((), ())),
        preferred_element_type=f32,
    )
    cells = main.shape[0] // PATCH
    main[...] = ext[OV * cells : (OV + PATCH) * cells]
    down[...] = ext[: OV * cells].astype(bf16)
    up[...] = ext[(OV + PATCH) * cells :].astype(bf16)


def decode(pos, total, o3, n3, f3, w_dec):
    rows, width = total.shape
    wide = w_dec.shape[0]
    cells = wide // (PATCH + 2 * OV)
    vmem = pl.BlockSpec(memory_space=pltpu.VMEM)
    edge = jax.ShapeDtypeStruct((OV * cells, rows), bf16)
    return pl.pallas_call(
        decode_kernel,
        in_specs=[pl.BlockSpec(memory_space=pltpu.SMEM)] + [vmem] * 5,
        out_specs=[vmem] * 3,
        out_shape=[jax.ShapeDtypeStruct((PATCH * cells, rows), f32), edge, edge],
        scratch_shapes=[
            pltpu.VMEM((rows, n3.shape[0] + f3.shape[0]), bf16),
            pltpu.VMEM((rows, width), f32),
        ],
        compiler_params=pltpu.CompilerParams(vmem_limit_bytes=12 * 2**20),
        name="decode",
    )(pos, total, o3, n3, f3, w_dec)


def gathered_kernel(*refs):
    rows = refs[0].shape[0]
    for i, part in enumerate(refs[:-1]):
        refs[-1][pl.ds(i * rows, rows)] = part[...]


def gathered(parts):
    rows, width = parts[0].shape
    vmem = pl.BlockSpec(memory_space=pltpu.VMEM)
    return pl.pallas_call(
        gathered_kernel,
        in_specs=[vmem] * len(parts),
        out_specs=vmem,
        out_shape=jax.ShapeDtypeStruct((len(parts) * rows, width), bf16),
        compiler_params=pltpu.CompilerParams(vmem_limit_bytes=4 * 2**20),
        name="gathered",
    )(*parts)


def first_way(value):
    count = lax.axis_size("ctx") * lax.axis_size("head")
    pairs = [(i, i ^ (1 if (i // 4) % 2 == 0 else 2)) for i in range(count)]
    return lax.ppermute(value, ("ctx", "head"), pairs)


def second_way(value):
    count = lax.axis_size("ctx") * lax.axis_size("head")
    pairs = [(i, i ^ (2 if (i // 4) % 2 == 0 else 1)) for i in range(count)]
    return lax.ppermute(value, ("ctx", "head"), pairs)


def fast_body(tokens, w_qkv, w_out, w_dec):
    rows = tokens.shape[0]
    ctx = lax.axis_index("ctx")
    pos = jnp.stack([ctx // 2, ctx % 2])

    p0, p1, p2, p3, half = project(pos, tokens, w_qkv, w_out)
    r2, r3, r1 = swapped(p2, "ctx", 4), swapped(p3, "ctx", 6), swapped(p1, "ctx", 2)


    n1, n2 = first_way(half), second_way(half)
    c0, c1, c2, c3 = (swapped(part, "ctx", 1) for part in (p0, r1, r2, r3))
    n1, n2, c0, c1, c2, c3 = lax.optimization_barrier((n1, n2, c0, c1, c2, c3))
    n3 = second_way(n1)

    o2, o3 = attend([r2, r3, p0, r1, c0, c1, c2, c3])
    o0, o1 = attend([p0, r1, r2, r3, c0, c1, c2, c3])
    own = gathered([o0, swapped(o1, "ctx", 2), swapped(o2, "ctx", 4), swapped(o3, "ctx", 6)])
    own, n1, n2 = lax.optimization_barrier((own, n1, n2))
    a1, a2 = first_way(own), second_way(own)
    f1, f2 = (swapped(part, "ctx", 1) for part in (n1, n2))
    a1, n3 = lax.optimization_barrier((a1, n3))
    a3 = second_way(a1)
    f3 = swapped(n3, "ctx", 1)
    total = mix(pos, tokens, [own, a1, a2], [w_out, n1, f2, n2, f1])

    dec = w_dec.transpose(1, 2, 0)
    dec = dec.reshape(-1, dec.shape[2])
    main, up, down = decode(pos, total, a3, n3, f3, dec)
    from_before = passed_along(up, "ctx", 1).astype(f32)
    from_after = passed_along(down, "ctx", -1).astype(f32)
    edge = up.shape[0]
    field = jnp.concatenate(
        [main[:edge] + from_before, main[edge:-edge], main[-edge:] + from_after], axis=0
    )
    return field.reshape(PATCH, -1, rows).transpose(2, 0, 1)


def general_body(tokens, w_qkv, w_out, w_dec):
    rows = tokens.shape[0]
    local_heads = w_qkv.shape[2] // HD
    xf = tokens.astype(f32)
    normed = rms_scale(xf).astype(bf16)
    projected = jnp.einsum("td,kdc->ktc", normed, w_qkv, preferred_element_type=f32).astype(bf16)
    queries = projected[0].reshape(rows, local_heads, HD)
    keyvals = projected[1:]
    scale = HD ** (-0.5)

    def block_update(carry, block):
        best, total, accum = carry
        keys = block[0].reshape(-1, local_heads, HD)
        values = block[1].reshape(-1, local_heads, HD)
        scores = jnp.einsum("thd,rhd->thr", queries, keys, preferred_element_type=f32) * scale
        fresh = jnp.maximum(best, jnp.max(scores, axis=-1))
        shrink = jnp.exp(best - fresh)
        weights = jnp.exp(scores - fresh[..., None])
        total = total * shrink + jnp.sum(weights, axis=-1)
        accum = accum * shrink[..., None] + jnp.einsum(
            "thr,rhd->thd", weights.astype(bf16), values, preferred_element_type=f32
        )
        return (fresh, total, accum)

    initial = (
        jnp.full((rows, local_heads), -1e30, f32),
        jnp.zeros((rows, local_heads), f32),
        jnp.zeros((rows, local_heads, HD), f32),
    )
    piece = lax.all_gather(keyvals, "ctx", axis=1, tiled=True)
    length = piece.shape[1]
    span = math.gcd(length, 1024)

    def one_block(index, inner):
        block = lax.dynamic_slice_in_dim(piece, index * span, span, 1)
        return block_update(inner, block)

    best, total, accum = lax.fori_loop(0, length // span, one_block, initial)
    attended = (accum / total[..., None]).astype(bf16).reshape(rows, local_heads * HD)
    partial_out = jnp.dot(attended, w_out, preferred_element_type=f32)
    mixed = lax.psum(partial_out.astype(bf16), "head").astype(f32)
    hidden = rms_scale(xf + mixed).astype(bf16)
    extended = jnp.dot(hidden, w_dec.reshape(w_dec.shape[0], -1), preferred_element_type=f32)
    extended = extended.reshape(rows, w_dec.shape[1], w_dec.shape[2])
    from_before = passed_along(extended[:, PATCH + OV :].astype(bf16), "ctx", 1).astype(f32)
    from_after = passed_along(extended[:, :OV].astype(bf16), "ctx", -1).astype(f32)
    middle = extended[:, OV : OV + PATCH]
    return jnp.concatenate(
        [
            middle[:, :OV] + from_before,
            middle[:, OV : PATCH - OV],
            middle[:, PATCH - OV :] + from_after,
        ],
        axis=1,
    )


def body(tokens, w_qkv, w_out, w_dec):
    fits = lax.axis_size("ctx") == 8 and lax.axis_size("head") == 4
    fits = fits and w_qkv.shape[2] == 4 * LANES and tokens.shape[0] % 256 == 0
    run = fast_body if fits else general_body
    return run(tokens, w_qkv, w_out, w_dec)


def solution(mesh):
    return jax.shard_map(
        body,
        mesh=mesh,
        in_specs=(P("ctx", None), P(None, None, "head"), P("head", None), P(None, None, "head")),
        out_specs=P("ctx", None, "head"),
        check_vma=False,
    )
```

```python
import functools
import math

import jax
import jax.numpy as jnp
from jax import lax
from jax.experimental import pallas as pl
from jax.experimental.pallas import tpu as pltpu
from jax.sharding import PartitionSpec as P

HD = 64
PATCH = 8
OV = 2
LANES = 128

eps = 1e-05
bf16 = jnp.bfloat16
f32 = jnp.float32


def passed_along(value, axis, steps):
    count = lax.axis_size(axis)
    pairs = [(source, (source + steps) % count) for source in range(count)]
    return lax.ppermute(value, axis, pairs)


def swapped(value, axis, bits):
    count = lax.axis_size(axis)
    return lax.ppermute(value, axis, [(i, i ^ bits) for i in range(count)])


def rms_scale(values):
    return values * lax.rsqrt(jnp.mean(values * values, axis=-1, keepdims=True) + eps)


def project_kernel(pos, x_hbm, w_hbm, out_hbm, *refs):
    packs, half_ref = refs[:4], refs[4]
    x_ref, w_ref, x_sem, w_sem, half_sem = refs[5:]
    z, core = pos[0], pos[1]
    rows = x_ref.shape[0]
    pairs = [(z // 2) ^ 1, z // 2]
    copies = []
    for i, pair in enumerate(pairs):
        for k in range(3):
            cols = pl.ds(pl.multiple_of(pair * 2 * LANES, 2 * LANES), 2 * LANES)
            n = 3 * i + k
            copies.append(pltpu.make_async_copy(w_hbm.at[k, :, cols], w_ref.at[n], w_sem.at[n]))
    x_copy = pltpu.make_async_copy(x_hbm, x_ref, x_sem)
    x_copy.start()
    for copy in copies:
        copy.start()
    half = half_ref.shape[0]
    half_copy = pltpu.make_async_copy(
        out_hbm.at[pl.ds(pl.multiple_of(core * half, half), half)], half_ref, half_sem
    )
    half_copy.start()
    x_copy.wait()
    x = x_ref[...].astype(f32)
    scale = lax.rsqrt(jnp.mean(x * x, axis=-1, keepdims=True) + eps)
    q_scale = scale * (HD ** (-0.5) * math.log2(math.e))
    odd = z % 2
    for i in range(2):
        even_pack, odd_pack = packs[2 * (1 - i)], packs[2 * (1 - i) + 1]
        for k in range(3):
            copies[3 * i + k].wait()
            out = jnp.dot(x_ref[...], w_ref[3 * i + k], preferred_element_type=f32)
            out = (out * (q_scale if k == 0 else scale)).astype(bf16)
            left, right = out[:, :LANES], out[:, LANES:]
            part = pl.ds(k * rows, rows)
            even_pack[part] = jnp.where(odd == 0, left, right)
            odd_pack[part] = jnp.where(odd == 0, right, left)
    half_copy.wait()


def project(pos, tokens, w_qkv, w_out):
    rows, width = tokens.shape
    hbm = pl.BlockSpec(memory_space=pltpu.HBM)
    vmem = pl.BlockSpec(memory_space=pltpu.VMEM)
    pack = jax.ShapeDtypeStruct((3 * rows, LANES), bf16)
    return pl.pallas_call(
        project_kernel,
        in_specs=[pl.BlockSpec(memory_space=pltpu.SMEM), hbm, hbm, hbm],
        out_specs=[vmem] * 5,
        out_shape=[pack] * 4 + [jax.ShapeDtypeStruct((w_out.shape[0] // 2, width), bf16)],
        scratch_shapes=[
            pltpu.VMEM((rows, width), bf16),
            pltpu.VMEM((6, width, 2 * LANES), bf16),
            pltpu.SemaphoreType.DMA(()),
            pltpu.SemaphoreType.DMA((6,)),
            pltpu.SemaphoreType.DMA(()),
        ],
        compiler_params=pltpu.CompilerParams(vmem_limit_bytes=60 * 2**20),
        name="project",
    )(pos, tokens, w_qkv, w_out)


def attention_kernel(*refs):
    packs, outs = refs[:8], refs[8:10]
    k_all, v_lo, v_hi, q_all = refs[10:]
    rows = packs[0].shape[0] // 3
    low = lax.broadcasted_iota(jnp.int32, (1, LANES), 1) < HD
    one = jnp.ones((), bf16)
    zero = jnp.zeros((), bf16)
    for i, pack in enumerate(packs):
        part = pl.ds(i * rows, rows)
        k_all[part] = pack[rows : 2 * rows]
        v = pack[2 * rows :]
        v_lo[part] = jnp.where(low, v, one)
        v_hi[part] = jnp.where(low, one, v)
    for i in range(2):
        q_all[pl.ds(i * rows, rows)] = packs[i][:rows]

    def score(q):
        return lax.dot_general(
            q, k_all[...], (((1,), (1,)), ((), ())), preferred_element_type=f32
        )

    def weigh(scores):
        return jnp.exp2(scores - jnp.max(scores, axis=-1, keepdims=True)).astype(bf16)

    q = q_all[...]
    lo_scores = score(jnp.where(low, q, zero))
    hi_scores = score(jnp.where(low, zero, q))
    lo_weights, hi_weights = weigh(lo_scores), weigh(hi_scores)
    lo = jnp.dot(lo_weights, v_lo[...], preferred_element_type=f32)
    hi = jnp.dot(hi_weights, v_hi[...], preferred_element_type=f32)
    top = jnp.where(low, lo, hi)
    bottom = pltpu.roll(jnp.where(low, hi, lo), HD, 1)
    attended = (top / bottom).astype(bf16)
    for i in range(2):
        outs[i][...] = attended[i * rows : (i + 1) * rows]


def attend(packs):
    rows = packs[0].shape[0] // 3
    keys = rows * len(packs)
    vmem = pl.BlockSpec(memory_space=pltpu.VMEM)
    return pl.pallas_call(
        attention_kernel,
        in_specs=[vmem] * len(packs),
        out_specs=[vmem] * 2,
        out_shape=[jax.ShapeDtypeStruct((rows, LANES), bf16)] * 2,
        scratch_shapes=[pltpu.VMEM((keys, LANES), bf16)] * 3 + [pltpu.VMEM((2 * rows, LANES), bf16)],
        compiler_params=pltpu.CompilerParams(vmem_limit_bytes=24 * 2**20),
        name="attend",
    )(*packs)


def mix_kernel(pos, x_ref, o0, o1, o2, own, n1, f2, n2, f1, total, att):
    z, core = pos[0], pos[1]
    rows, width = x_ref.shape
    local = own.shape[0]
    for s in range(4):
        place = z ^ s
        part = pl.ds(s * rows, rows)
        att[:, pl.ds(pl.multiple_of(place * LANES, LANES), LANES)] = o0[part]
        place = place ^ (2 * core)
        for i, o in enumerate((o1, o2)):
            at = pl.multiple_of((i + 1) * local + place * LANES, LANES)
            att[:, pl.ds(at, LANES)] = o[part]
    step = 512
    for n in range(0, width, step):
        w = jnp.concatenate([part[:, n : n + step] for part in (own, n1, f2, n2, f1)], axis=0)
        mixed = jnp.dot(att[...], w, preferred_element_type=f32)
        total[:, n : n + step] = x_ref[:, n : n + step].astype(f32) + mixed


def mix(pos, tokens, outs, parts):
    rows, width = tokens.shape
    vmem = pl.BlockSpec(memory_space=pltpu.VMEM)
    return pl.pallas_call(
        mix_kernel,
        in_specs=[pl.BlockSpec(memory_space=pltpu.SMEM)] + [vmem] * 9,
        out_specs=vmem,
        out_shape=jax.ShapeDtypeStruct((rows, width), f32),
        scratch_shapes=[pltpu.VMEM((rows, 3 * parts[0].shape[0]), bf16)],
        compiler_params=pltpu.CompilerParams(vmem_limit_bytes=12 * 2**20),
        name="mix",
    )(pos, tokens, *outs, *parts)


def decode_kernel(pos, total, o3, n3, f3, dec_ref, main, up, down, att, hidden):
    z, core = pos[0], pos[1]
    rows, width = total.shape
    for s in range(4):
        place = z ^ s ^ (2 * core)
        att[:, pl.ds(pl.multiple_of(place * LANES, LANES), LANES)] = o3[pl.ds(s * rows, rows)]
    step = 512
    squares = jnp.zeros((rows, LANES), f32)
    for n in range(0, width, step):
        w = jnp.concatenate([part[:, n : n + step] for part in (n3, f3)], axis=0)
        mixed = total[:, n : n + step] + jnp.dot(att[...], w, preferred_element_type=f32)
        hidden[:, n : n + step] = mixed
        for i in range(0, step, LANES):
            squares += mixed[:, i : i + LANES] * mixed[:, i : i + LANES]
    scale = lax.rsqrt(jnp.sum(squares, axis=-1, keepdims=True) * (1.0 / width) + eps)
    ext = lax.dot_general(
        dec_ref[...],
        (hidden[...] * scale).astype(bf16),
        (((1,), (1,)), ((), ())),
        preferred_element_type=f32,
    )
    cells = main.shape[0] // PATCH
    main[...] = ext[OV * cells : (OV + PATCH) * cells]
    down[...] = ext[: OV * cells].astype(bf16)
    up[...] = ext[(OV + PATCH) * cells :].astype(bf16)


def decode(pos, total, o3, n3, f3, w_dec):
    rows, width = total.shape
    wide = w_dec.shape[0]
    cells = wide // (PATCH + 2 * OV)
    vmem = pl.BlockSpec(memory_space=pltpu.VMEM)
    edge = jax.ShapeDtypeStruct((OV * cells, rows), bf16)
    return pl.pallas_call(
        decode_kernel,
        in_specs=[pl.BlockSpec(memory_space=pltpu.SMEM)] + [vmem] * 5,
        out_specs=[vmem] * 3,
        out_shape=[jax.ShapeDtypeStruct((PATCH * cells, rows), f32), edge, edge],
        scratch_shapes=[
            pltpu.VMEM((rows, n3.shape[0] + f3.shape[0]), bf16),
            pltpu.VMEM((rows, width), f32),
        ],
        compiler_params=pltpu.CompilerParams(vmem_limit_bytes=12 * 2**20),
        name="decode",
    )(pos, total, o3, n3, f3, w_dec)


def gathered_kernel(*refs):
    rows = refs[0].shape[0]
    for i, part in enumerate(refs[:-1]):
        refs[-1][pl.ds(i * rows, rows)] = part[...]


def gathered(parts):
    rows, width = parts[0].shape
    vmem = pl.BlockSpec(memory_space=pltpu.VMEM)
    return pl.pallas_call(
        gathered_kernel,
        in_specs=[vmem] * len(parts),
        out_specs=vmem,
        out_shape=jax.ShapeDtypeStruct((len(parts) * rows, width), bf16),
        compiler_params=pltpu.CompilerParams(vmem_limit_bytes=4 * 2**20),
        name="gathered",
    )(*parts)


def first_way(value):
    count = lax.axis_size("ctx") * lax.axis_size("head")
    pairs = [(i, i ^ (1 if (i // 4) % 2 == 0 else 2)) for i in range(count)]
    return lax.ppermute(value, ("ctx", "head"), pairs)


def second_way(value):
    count = lax.axis_size("ctx") * lax.axis_size("head")
    pairs = [(i, i ^ (2 if (i // 4) % 2 == 0 else 1)) for i in range(count)]
    return lax.ppermute(value, ("ctx", "head"), pairs)


def fast_body(tokens, w_qkv, w_out, w_dec):
    rows = tokens.shape[0]
    ctx = lax.axis_index("ctx")
    pos = jnp.stack([ctx // 2, ctx % 2])

    p0, p1, p2, p3, half = project(pos, tokens, w_qkv, w_out)
    r2, r3, r1 = swapped(p2, "ctx", 4), swapped(p3, "ctx", 6), swapped(p1, "ctx", 2)


    n1, n2 = first_way(half), second_way(half)
    c0, c1, c2, c3 = (swapped(part, "ctx", 1) for part in (p0, r1, r2, r3))
    n1, n2, c0, c1, c2, c3 = lax.optimization_barrier((n1, n2, c0, c1, c2, c3))
    n3 = second_way(n1)

    o2, o3 = attend([r2, r3, p0, r1, c0, c1, c2, c3])
    o0, o1 = attend([p0, r1, r2, r3, c0, c1, c2, c3])
    own = gathered([o0, swapped(o1, "ctx", 2), swapped(o2, "ctx", 4), swapped(o3, "ctx", 6)])
    own, n1, n2 = lax.optimization_barrier((own, n1, n2))
    a1, a2 = first_way(own), second_way(own)
    f1, f2 = (swapped(part, "ctx", 1) for part in (n1, n2))
    a1, n3 = lax.optimization_barrier((a1, n3))
    a3 = second_way(a1)
    f3 = swapped(n3, "ctx", 1)
    total = mix(pos, tokens, [own, a1, a2], [w_out, n1, f2, n2, f1])

    dec = w_dec.transpose(1, 2, 0)
    dec = dec.reshape(-1, dec.shape[2])
    main, up, down = decode(pos, total, a3, n3, f3, dec)
    from_before = passed_along(up, "ctx", 1).astype(f32)
    from_after = passed_along(down, "ctx", -1).astype(f32)
    edge = up.shape[0]
    field = jnp.concatenate(
        [main[:edge] + from_before, main[edge:-edge], main[-edge:] + from_after], axis=0
    )
    return field.reshape(PATCH, -1, rows).transpose(2, 0, 1)


def general_body(tokens, w_qkv, w_out, w_dec):
    rows = tokens.shape[0]
    local_heads = w_qkv.shape[2] // HD
    xf = tokens.astype(f32)
    normed = rms_scale(xf).astype(bf16)
    projected = jnp.einsum("td,kdc->ktc", normed, w_qkv, preferred_element_type=f32).astype(bf16)
    queries = projected[0].reshape(rows, local_heads, HD)
    keyvals = projected[1:]
    scale = HD ** (-0.5)

    def block_update(carry, block):
        best, total, accum = carry
        keys = block[0].reshape(-1, local_heads, HD)
        values = block[1].reshape(-1, local_heads, HD)
        scores = jnp.einsum("thd,rhd->thr", queries, keys, preferred_element_type=f32) * scale
        fresh = jnp.maximum(best, jnp.max(scores, axis=-1))
        shrink = jnp.exp(best - fresh)
        weights = jnp.exp(scores - fresh[..., None])
        total = total * shrink + jnp.sum(weights, axis=-1)
        accum = accum * shrink[..., None] + jnp.einsum(
            "thr,rhd->thd", weights.astype(bf16), values, preferred_element_type=f32
        )
        return (fresh, total, accum)

    initial = (
        jnp.full((rows, local_heads), -1e30, f32),
        jnp.zeros((rows, local_heads), f32),
        jnp.zeros((rows, local_heads, HD), f32),
    )
    piece = lax.all_gather(keyvals, "ctx", axis=1, tiled=True)
    length = piece.shape[1]
    span = math.gcd(length, 1024)

    def one_block(index, inner):
        block = lax.dynamic_slice_in_dim(piece, index * span, span, 1)
        return block_update(inner, block)

    best, total, accum = lax.fori_loop(0, length // span, one_block, initial)
    attended = (accum / total[..., None]).astype(bf16).reshape(rows, local_heads * HD)
    partial_out = jnp.dot(attended, w_out, preferred_element_type=f32)
    mixed = lax.psum(partial_out.astype(bf16), "head").astype(f32)
    hidden = rms_scale(xf + mixed).astype(bf16)
    extended = jnp.dot(hidden, w_dec.reshape(w_dec.shape[0], -1), preferred_element_type=f32)
    extended = extended.reshape(rows, w_dec.shape[1], w_dec.shape[2])
    from_before = passed_along(extended[:, PATCH + OV :].astype(bf16), "ctx", 1).astype(f32)
    from_after = passed_along(extended[:, :OV].astype(bf16), "ctx", -1).astype(f32)
    middle = extended[:, OV : OV + PATCH]
    return jnp.concatenate(
        [
            middle[:, :OV] + from_before,
            middle[:, OV : PATCH - OV],
            middle[:, PATCH - OV :] + from_after,
        ],
        axis=1,
    )


def body(tokens, w_qkv, w_out, w_dec):
    fits = lax.axis_size("ctx") == 8 and lax.axis_size("head") == 4
    fits = fits and w_qkv.shape[2] == 4 * LANES and tokens.shape[0] % 256 == 0
    run = fast_body if fits else general_body
    return run(tokens, w_qkv, w_out, w_dec)


def solution(mesh):
    return jax.shard_map(
        body,
        mesh=mesh,
        in_specs=(P("ctx", None), P(None, None, "head"), P("head", None), P(None, None, "head")),
        out_specs=P("ctx", None, "head"),
        check_vma=False,
    )
```

```python
import functools
import math

import jax
import jax.numpy as jnp
from jax import lax
from jax.experimental import pallas as pl
from jax.experimental.pallas import tpu as pltpu
from jax.sharding import PartitionSpec as P

HD = 64
PATCH = 8
OV = 2
LANES = 128

eps = 1e-05
bf16 = jnp.bfloat16
f32 = jnp.float32


def passed_along(value, axis, steps):
    count = lax.axis_size(axis)
    pairs = [(source, (source + steps) % count) for source in range(count)]
    return lax.ppermute(value, axis, pairs)


def swapped(value, axis, bits):
    count = lax.axis_size(axis)
    return lax.ppermute(value, axis, [(i, i ^ bits) for i in range(count)])


def rms_scale(values):
    return values * lax.rsqrt(jnp.mean(values * values, axis=-1, keepdims=True) + eps)


def place():
    ctx = lax.axis_index("ctx")
    return lax.div(ctx, 2), lax.rem(ctx, 2)


def project_kernel(x_ref, w_hbm, *refs):
    packs = refs[:5]
    w_ref, w_sem = refs[5:]
    z, _ = place()
    rows = x_ref.shape[0]
    copies = [pltpu.make_async_copy(w_hbm.at[k], w_ref.at[k], w_sem.at[k]) for k in range(3)]
    for copy in copies:
        copy.start()
    x = x_ref[...].astype(f32)
    scale = lax.rsqrt(jnp.mean(x * x, axis=-1, keepdims=True) + eps)
    q_scale = scale * (HD ** (-0.5) * math.log2(math.e))
    odd = lax.rem(z, 2) == 1
    upper = lax.div(z, 2) == 1
    for k, copy in enumerate(copies):
        copy.wait()
        out = jnp.dot(x_ref[...], w_ref[k], preferred_element_type=f32)
        out = (out * (q_scale if k == 0 else scale)).astype(bf16)
        parts = [out[:, i * LANES : (i + 1) * LANES] for i in range(4)]
        parts = [jnp.where(odd, parts[i ^ 1], parts[i]) for i in range(4)]
        parts = [jnp.where(upper, parts[i ^ 2], parts[i]) for i in range(4)]
        for pack, part in zip(packs, parts):
            pack[pl.ds(k * rows, rows)] = part
    packs[4][...] = packs[0][...]


def project(tokens, w_qkv):
    rows = tokens.shape[0]
    vmem = pl.BlockSpec(memory_space=pltpu.VMEM)
    return pl.pallas_call(
        project_kernel,
        in_specs=[vmem, pl.BlockSpec(memory_space=pltpu.HBM)],
        out_specs=[vmem] * 5,
        out_shape=[jax.ShapeDtypeStruct((3 * rows, LANES), bf16)] * 5,
        scratch_shapes=[pltpu.VMEM(w_qkv.shape, bf16), pltpu.SemaphoreType.DMA((3,))],
        compiler_params=pltpu.CompilerParams(vmem_limit_bytes=52 * 2**20),
        name="project",
    )(tokens, w_qkv)


def attention_kernel(*refs):
    packs, outs = refs[:8], refs[8:10]
    k_all, v_lo, v_hi, q_all = refs[10:]
    rows = packs[0].shape[0] // 3
    low = lax.broadcasted_iota(jnp.int32, (1, LANES), 1) < HD
    one = jnp.ones((), bf16)
    zero = jnp.zeros((), bf16)
    for i, pack in enumerate(packs):
        part = pl.ds(i * rows, rows)
        k_all[part] = pack[rows : 2 * rows]
        v = pack[2 * rows :]
        v_lo[part] = jnp.where(low, v, one)
        v_hi[part] = jnp.where(low, one, v)
    for i in range(2):
        q_all[pl.ds(i * rows, rows)] = packs[i][:rows]

    def score(q):
        return lax.dot_general(
            q, k_all[...], (((1,), (1,)), ((), ())), preferred_element_type=f32
        )

    def weigh(scores):
        return jnp.exp2(scores - jnp.max(scores, axis=-1, keepdims=True)).astype(bf16)

    q = q_all[...]
    lo_scores = score(jnp.where(low, q, zero))
    hi_scores = score(jnp.where(low, zero, q))
    lo_weights, hi_weights = weigh(lo_scores), weigh(hi_scores)
    lo = jnp.dot(lo_weights, v_lo[...], preferred_element_type=f32)
    hi = jnp.dot(hi_weights, v_hi[...], preferred_element_type=f32)
    top = jnp.where(low, lo, hi)
    bottom = pltpu.roll(jnp.where(low, hi, lo), HD, 1)
    attended = (top / bottom).astype(bf16)
    for i in range(2):
        outs[i][...] = attended[i * rows : (i + 1) * rows]


def attend(packs):
    rows = packs[0].shape[0] // 3
    keys = rows * len(packs)
    vmem = pl.BlockSpec(memory_space=pltpu.VMEM)
    return pl.pallas_call(
        attention_kernel,
        in_specs=[vmem] * len(packs),
        out_specs=[vmem] * 2,
        out_shape=[jax.ShapeDtypeStruct((rows, LANES), bf16)] * 2,
        scratch_shapes=[pltpu.VMEM((keys, LANES), bf16)] * 3 + [pltpu.VMEM((2 * rows, LANES), bf16)],
        compiler_params=pltpu.CompilerParams(vmem_limit_bytes=24 * 2**20),
        name="attend",
    )(*packs)


def mix_kernel(x_ref, o0, o1, o2, own, n1, f2, n2, f1, total, att):
    z, core = place()
    rows, width = x_ref.shape
    local = own.shape[0]
    for s in range(4):
        spot = z ^ s
        part = pl.ds(s * rows, rows)
        att[:, pl.ds(pl.multiple_of(spot * LANES, LANES), LANES)] = o0[part]
        spot = spot ^ (2 * core)
        for i, o in enumerate((o1, o2)):
            at = pl.multiple_of((i + 1) * local + spot * LANES, LANES)
            att[:, pl.ds(at, LANES)] = o[part]
    step = 512
    for n in range(0, width, step):
        w = jnp.concatenate([part[:, n : n + step] for part in (own, n1, f2, n2, f1)], axis=0)
        mixed = jnp.dot(att[...], w, preferred_element_type=f32)
        total[:, n : n + step] = x_ref[:, n : n + step].astype(f32) + mixed


def mix(tokens, outs, parts):
    rows, width = tokens.shape
    vmem = pl.BlockSpec(memory_space=pltpu.VMEM)
    return pl.pallas_call(
        mix_kernel,
        in_specs=[vmem] * 9,
        out_specs=vmem,
        out_shape=jax.ShapeDtypeStruct((rows, width), f32),
        scratch_shapes=[pltpu.VMEM((rows, 3 * parts[0].shape[0]), bf16)],
        compiler_params=pltpu.CompilerParams(vmem_limit_bytes=12 * 2**20),
        name="mix",
    )(tokens, *outs, *parts)


def edges_kernel(total, o3, n3, f3, dec_ref, hidden, inner, outer, att, held):
    z, core = place()
    rows, width = total.shape
    for s in range(4):
        spot = z ^ s ^ (2 * core)
        att[:, pl.ds(pl.multiple_of(spot * LANES, LANES), LANES)] = o3[pl.ds(s * rows, rows)]
    step = 512
    squares = jnp.zeros((rows, LANES), f32)
    for n in range(0, width, step):
        w = jnp.concatenate([part[:, n : n + step] for part in (n3, f3)], axis=0)
        mixed = total[:, n : n + step] + jnp.dot(att[...], w, preferred_element_type=f32)
        held[:, n : n + step] = mixed
        for i in range(0, step, LANES):
            squares += mixed[:, i : i + LANES] * mixed[:, i : i + LANES]
    scale = lax.rsqrt(jnp.sum(squares, axis=-1, keepdims=True) * (1.0 / width) + eps)
    hidden[...] = (held[...] * scale).astype(bf16)
    edge = inner.shape[0]
    last = dec_ref.shape[0] - edge

    def cells(part):
        return lax.dot_general(
            dec_ref[part], hidden[...], (((1,), (1,)), ((), ())), preferred_element_type=f32
        ).astype(bf16)

    down = cells(pl.ds(0, edge))
    up = cells(pl.ds(last, edge))
    inner[...] = jnp.where(core == 0, up, down)
    outer[...] = jnp.where(core == 0, down, up)


def decode_edges(total, o3, n3, f3, w_dec):
    rows, width = total.shape
    cells = w_dec.shape[0] // (PATCH + 2 * OV)
    vmem = pl.BlockSpec(memory_space=pltpu.VMEM)
    edge = jax.ShapeDtypeStruct((OV * cells, rows), bf16)
    return pl.pallas_call(
        edges_kernel,
        in_specs=[vmem] * 5,
        out_specs=[vmem] * 3,
        out_shape=[jax.ShapeDtypeStruct((rows, width), bf16), edge, edge],
        scratch_shapes=[
            pltpu.VMEM((rows, n3.shape[0] + f3.shape[0]), bf16),
            pltpu.VMEM((rows, width), f32),
        ],
        compiler_params=pltpu.CompilerParams(vmem_limit_bytes=12 * 2**20),
        name="decode_edges",
    )(total, o3, n3, f3, w_dec)


def main_kernel(hidden, dec_ref, main):
    edge = (dec_ref.shape[0] - main.shape[0]) // 2
    main[...] = lax.dot_general(
        dec_ref[pl.ds(edge, main.shape[0])],
        hidden[...],
        (((1,), (1,)), ((), ())),
        preferred_element_type=f32,
    )


def decode_main(hidden, w_dec):
    cells = w_dec.shape[0] // (PATCH + 2 * OV)
    vmem = pl.BlockSpec(memory_space=pltpu.VMEM)
    return pl.pallas_call(
        main_kernel,
        in_specs=[vmem] * 2,
        out_specs=vmem,
        out_shape=jax.ShapeDtypeStruct((PATCH * cells, hidden.shape[0]), f32),
        compiler_params=pltpu.CompilerParams(vmem_limit_bytes=8 * 2**20),
        name="decode_main",
    )(hidden, w_dec)


def join_kernel(main, inner, outer, field):
    _, core = place()
    edge = inner.shape[0]
    rest = main.shape[0] - edge
    before = jnp.where(core == 0, outer[...], inner[...]).astype(f32)
    after = jnp.where(core == 0, inner[...], outer[...]).astype(f32)
    field[:edge] = main[:edge] + before
    field[edge:rest] = main[edge:rest]
    field[rest:] = main[rest:] + after


def join(main, inner, outer):
    vmem = pl.BlockSpec(memory_space=pltpu.VMEM)
    return pl.pallas_call(
        join_kernel,
        in_specs=[vmem] * 3,
        out_specs=vmem,
        out_shape=jax.ShapeDtypeStruct(main.shape, f32),
        compiler_params=pltpu.CompilerParams(vmem_limit_bytes=4 * 2**20),
        name="join",
    )(main, inner, outer)


def gathered_kernel(*refs):
    rows = refs[0].shape[0]
    for i, part in enumerate(refs[:-1]):
        refs[-1][pl.ds(i * rows, rows)] = part[...]


def gathered(parts):
    rows, width = parts[0].shape
    vmem = pl.BlockSpec(memory_space=pltpu.VMEM)
    return pl.pallas_call(
        gathered_kernel,
        in_specs=[vmem] * len(parts),
        out_specs=vmem,
        out_shape=jax.ShapeDtypeStruct((len(parts) * rows, width), bf16),
        compiler_params=pltpu.CompilerParams(vmem_limit_bytes=4 * 2**20),
        name="gathered",
    )(*parts)


def first_way(value):
    count = lax.axis_size("ctx") * lax.axis_size("head")
    pairs = [(i, i ^ (1 if (i // 4) % 2 == 0 else 2)) for i in range(count)]
    return lax.ppermute(value, ("ctx", "head"), pairs)


def second_way(value):
    count = lax.axis_size("ctx") * lax.axis_size("head")
    pairs = [(i, i ^ (2 if (i // 4) % 2 == 0 else 1)) for i in range(count)]
    return lax.ppermute(value, ("ctx", "head"), pairs)


def fast_body(tokens, w_qkv, w_out, w_dec):
    rows = tokens.shape[0]

    size = w_out.shape[0] // 2
    half = lax.dynamic_slice_in_dim(w_out, lax.rem(lax.axis_index("ctx"), 2) * size, size, 0)
    n1, n2 = first_way(half), second_way(half)

    p0, p1, p2, p3, p0_sent = project(tokens, w_qkv)
    r2, r3, r1 = swapped(p2, "ctx", 4), swapped(p3, "ctx", 6), swapped(p1, "ctx", 2)
    c0, c1, c2, c3 = (swapped(part, "ctx", 1) for part in (p0_sent, r1, r2, r3))
    n1, n2, c0, c1, c2, c3 = lax.optimization_barrier((n1, n2, c0, c1, c2, c3))
    n3 = second_way(n1)

    o2, o3 = attend([r2, r3, p0, r1, c0, c1, c2, c3])
    o0, o1 = attend([p0, r1, r2, r3, c0, c1, c2, c3])
    own = gathered([o0, swapped(o1, "ctx", 2), swapped(o2, "ctx", 4), swapped(o3, "ctx", 6)])
    own, n1, n2 = lax.optimization_barrier((own, n1, n2))
    a1, a2 = first_way(own), second_way(own)
    f1, f2 = (swapped(part, "ctx", 1) for part in (n1, n2))
    a1, a2, n3 = lax.optimization_barrier((a1, a2, n3))
    a3 = second_way(a1)
    f3 = swapped(n3, "ctx", 1)
    total = mix(tokens, [own, a1, a2], [w_out, n1, f2, n2, f1])

    dec = w_dec.transpose(1, 2, 0)
    dec = dec.reshape(-1, dec.shape[2])
    hidden, inner, outer = decode_edges(total, a3, n3, f3, dec)
    count = lax.axis_size("ctx")
    pairs = [(i, (i - 1 + 2 * (i % 2)) % count) for i in range(count)]
    outer = lax.ppermute(outer, "ctx", pairs)
    inner = swapped(inner, "ctx", 1)
    field = join(decode_main(hidden, dec), inner, outer)
    return field.reshape(PATCH, -1, rows).transpose(2, 0, 1)


def general_body(tokens, w_qkv, w_out, w_dec):
    rows = tokens.shape[0]
    local_heads = w_qkv.shape[2] // HD
    xf = tokens.astype(f32)
    normed = rms_scale(xf).astype(bf16)
    projected = jnp.einsum("td,kdc->ktc", normed, w_qkv, preferred_element_type=f32).astype(bf16)
    queries = projected[0].reshape(rows, local_heads, HD)
    keyvals = projected[1:]
    scale = HD ** (-0.5)

    def block_update(carry, block):
        best, total, accum = carry
        keys = block[0].reshape(-1, local_heads, HD)
        values = block[1].reshape(-1, local_heads, HD)
        scores = jnp.einsum("thd,rhd->thr", queries, keys, preferred_element_type=f32) * scale
        fresh = jnp.maximum(best, jnp.max(scores, axis=-1))
        shrink = jnp.exp(best - fresh)
        weights = jnp.exp(scores - fresh[..., None])
        total = total * shrink + jnp.sum(weights, axis=-1)
        accum = accum * shrink[..., None] + jnp.einsum(
            "thr,rhd->thd", weights.astype(bf16), values, preferred_element_type=f32
        )
        return (fresh, total, accum)

    initial = (
        jnp.full((rows, local_heads), -1e30, f32),
        jnp.zeros((rows, local_heads), f32),
        jnp.zeros((rows, local_heads, HD), f32),
    )
    piece = lax.all_gather(keyvals, "ctx", axis=1, tiled=True)
    length = piece.shape[1]
    span = math.gcd(length, 1024)

    def one_block(index, inner):
        block = lax.dynamic_slice_in_dim(piece, index * span, span, 1)
        return block_update(inner, block)

    best, total, accum = lax.fori_loop(0, length // span, one_block, initial)
    attended = (accum / total[..., None]).astype(bf16).reshape(rows, local_heads * HD)
    partial_out = jnp.dot(attended, w_out, preferred_element_type=f32)
    mixed = lax.psum(partial_out.astype(bf16), "head").astype(f32)
    hidden = rms_scale(xf + mixed).astype(bf16)
    extended = jnp.dot(hidden, w_dec.reshape(w_dec.shape[0], -1), preferred_element_type=f32)
    extended = extended.reshape(rows, w_dec.shape[1], w_dec.shape[2])
    from_before = passed_along(extended[:, PATCH + OV :].astype(bf16), "ctx", 1).astype(f32)
    from_after = passed_along(extended[:, :OV].astype(bf16), "ctx", -1).astype(f32)
    middle = extended[:, OV : OV + PATCH]
    return jnp.concatenate(
        [
            middle[:, :OV] + from_before,
            middle[:, OV : PATCH - OV],
            middle[:, PATCH - OV :] + from_after,
        ],
        axis=1,
    )


def body(tokens, w_qkv, w_out, w_dec):
    fits = lax.axis_size("ctx") == 8 and lax.axis_size("head") == 4
    fits = fits and w_qkv.shape[2] == 4 * LANES and tokens.shape[0] % 256 == 0
    run = fast_body if fits else general_body
    return run(tokens, w_qkv, w_out, w_dec)


def solution(mesh):
    return jax.shard_map(
        body,
        mesh=mesh,
        in_specs=(P("ctx", None), P(None, None, "head"), P("head", None), P(None, None, "head")),
        out_specs=P("ctx", None, "head"),
        check_vma=False,
    )
```

```python
import functools
import math

import jax
import jax.numpy as jnp
from jax import lax
from jax.experimental import pallas as pl
from jax.experimental.pallas import tpu as pltpu
from jax.sharding import PartitionSpec as P

HD = 64
PATCH = 8
OV = 2
LANES = 128

eps = 1e-05
bf16 = jnp.bfloat16
f32 = jnp.float32


def passed_along(value, axis, steps):
    count = lax.axis_size(axis)
    pairs = [(source, (source + steps) % count) for source in range(count)]
    return lax.ppermute(value, axis, pairs)


def swapped(value, axis, bits):
    count = lax.axis_size(axis)
    return lax.ppermute(value, axis, [(i, i ^ bits) for i in range(count)])


def rms_scale(values):
    return values * lax.rsqrt(jnp.mean(values * values, axis=-1, keepdims=True) + eps)


def place():
    ctx = lax.axis_index("ctx")
    return lax.div(ctx, 2), lax.rem(ctx, 2)


def project_kernel(x_ref, w_hbm, *refs):
    packs = refs[:5]
    w_ref, w_sem = refs[5:]
    z, _ = place()
    rows = x_ref.shape[0]
    copies = [pltpu.make_async_copy(w_hbm.at[k], w_ref.at[k], w_sem.at[k]) for k in range(3)]
    for copy in copies:
        copy.start()
    x = x_ref[...].astype(f32)
    scale = lax.rsqrt(jnp.mean(x * x, axis=-1, keepdims=True) + eps)
    q_scale = scale * (HD ** (-0.5) * math.log2(math.e))
    odd = lax.rem(z, 2) == 1
    upper = lax.div(z, 2) == 1
    for k, copy in enumerate(copies):
        copy.wait()
        out = jnp.dot(x_ref[...], w_ref[k], preferred_element_type=f32)
        out = (out * (q_scale if k == 0 else scale)).astype(bf16)
        parts = [out[:, i * LANES : (i + 1) * LANES] for i in range(4)]
        parts = [jnp.where(odd, parts[i ^ 1], parts[i]) for i in range(4)]
        parts = [jnp.where(upper, parts[i ^ 2], parts[i]) for i in range(4)]
        for pack, part in zip(packs, parts):
            pack[pl.ds(k * rows, rows)] = part
    packs[4][...] = packs[0][...]


def project(tokens, w_qkv):
    rows = tokens.shape[0]
    vmem = pl.BlockSpec(memory_space=pltpu.VMEM)
    return pl.pallas_call(
        project_kernel,
        in_specs=[vmem, pl.BlockSpec(memory_space=pltpu.HBM)],
        out_specs=[vmem] * 5,
        out_shape=[jax.ShapeDtypeStruct((3 * rows, LANES), bf16)] * 5,
        scratch_shapes=[pltpu.VMEM(w_qkv.shape, bf16), pltpu.SemaphoreType.DMA((3,))],
        compiler_params=pltpu.CompilerParams(vmem_limit_bytes=52 * 2**20),
        name="project",
    )(tokens, w_qkv)


def attention_kernel(*refs):
    packs, outs = refs[:8], refs[8:10]
    k_all, v_lo, v_hi, q_all = refs[10:]
    rows = packs[0].shape[0] // 3
    low = lax.broadcasted_iota(jnp.int32, (1, LANES), 1) < HD
    one = jnp.ones((), bf16)
    zero = jnp.zeros((), bf16)
    for i, pack in enumerate(packs):
        part = pl.ds(i * rows, rows)
        k_all[part] = pack[rows : 2 * rows]
        v = pack[2 * rows :]
        v_lo[part] = jnp.where(low, v, one)
        v_hi[part] = jnp.where(low, one, v)
    for i in range(2):
        q_all[pl.ds(i * rows, rows)] = packs[i][:rows]

    def score(q):
        return lax.dot_general(
            q, k_all[...], (((1,), (1,)), ((), ())), preferred_element_type=f32
        )

    def weigh(scores):
        return jnp.exp2(scores - jnp.max(scores, axis=-1, keepdims=True)).astype(bf16)

    q = q_all[...]
    lo_scores = score(jnp.where(low, q, zero))
    hi_scores = score(jnp.where(low, zero, q))
    lo_weights, hi_weights = weigh(lo_scores), weigh(hi_scores)
    lo = jnp.dot(lo_weights, v_lo[...], preferred_element_type=f32)
    hi = jnp.dot(hi_weights, v_hi[...], preferred_element_type=f32)
    top = jnp.where(low, lo, hi)
    bottom = pltpu.roll(jnp.where(low, hi, lo), HD, 1)
    attended = (top / bottom).astype(bf16)
    for i in range(2):
        outs[i][...] = attended[i * rows : (i + 1) * rows]


def attend(packs):
    rows = packs[0].shape[0] // 3
    keys = rows * len(packs)
    vmem = pl.BlockSpec(memory_space=pltpu.VMEM)
    return pl.pallas_call(
        attention_kernel,
        in_specs=[vmem] * len(packs),
        out_specs=[vmem] * 2,
        out_shape=[jax.ShapeDtypeStruct((rows, LANES), bf16)] * 2,
        scratch_shapes=[pltpu.VMEM((keys, LANES), bf16)] * 3 + [pltpu.VMEM((2 * rows, LANES), bf16)],
        compiler_params=pltpu.CompilerParams(vmem_limit_bytes=24 * 2**20),
        name="attend",
    )(*packs)


def mix_kernel(x_ref, o0, o1, o2, own, w1, w2, total, att):
    z, _ = place()
    rows, width = x_ref.shape
    local = own.shape[0]
    for s in range(4):
        for i, o in enumerate((o0, o1, o2)):
            at = pl.multiple_of(i * local + (z ^ s) * LANES, LANES)
            att[:, pl.ds(at, LANES)] = o[pl.ds(s * rows, rows)]
    step = 512
    for n in range(0, width, step):
        w = jnp.concatenate([part[:, n : n + step] for part in (own, w1, w2)], axis=0)
        mixed = jnp.dot(att[...], w, preferred_element_type=f32)
        total[:, n : n + step] = x_ref[:, n : n + step].astype(f32) + mixed


def mix(tokens, outs, parts):
    rows, width = tokens.shape
    vmem = pl.BlockSpec(memory_space=pltpu.VMEM)
    return pl.pallas_call(
        mix_kernel,
        in_specs=[vmem] * 7,
        out_specs=vmem,
        out_shape=jax.ShapeDtypeStruct((rows, width), f32),
        scratch_shapes=[pltpu.VMEM((rows, 3 * parts[0].shape[0]), bf16)],
        compiler_params=pltpu.CompilerParams(vmem_limit_bytes=12 * 2**20),
        name="mix",
    )(tokens, *outs, *parts)


def edges_kernel(total, o3, n3, f3, dec_ref, hidden, inner, outer, att, held):
    z, core = place()
    rows, width = total.shape
    for s in range(4):
        spot = z ^ s ^ (2 * core)
        att[:, pl.ds(pl.multiple_of(spot * LANES, LANES), LANES)] = o3[pl.ds(s * rows, rows)]
    step = 512
    squares = jnp.zeros((rows, LANES), f32)
    for n in range(0, width, step):
        w = jnp.concatenate([part[:, n : n + step] for part in (n3, f3)], axis=0)
        mixed = total[:, n : n + step] + jnp.dot(att[...], w, preferred_element_type=f32)
        held[:, n : n + step] = mixed
        for i in range(0, step, LANES):
            squares += mixed[:, i : i + LANES] * mixed[:, i : i + LANES]
    scale = lax.rsqrt(jnp.sum(squares, axis=-1, keepdims=True) * (1.0 / width) + eps)
    hidden[...] = (held[...] * scale).astype(bf16)
    edge = inner.shape[0]
    last = dec_ref.shape[0] - edge

    def cells(part):
        return lax.dot_general(
            dec_ref[part], hidden[...], (((1,), (1,)), ((), ())), preferred_element_type=f32
        ).astype(bf16)

    down = cells(pl.ds(0, edge))
    up = cells(pl.ds(last, edge))
    inner[...] = jnp.where(core == 0, up, down)
    outer[...] = jnp.where(core == 0, down, up)


def decode_edges(total, o3, n3, f3, w_dec):
    rows, width = total.shape
    cells = w_dec.shape[0] // (PATCH + 2 * OV)
    vmem = pl.BlockSpec(memory_space=pltpu.VMEM)
    edge = jax.ShapeDtypeStruct((OV * cells, rows), bf16)
    return pl.pallas_call(
        edges_kernel,
        in_specs=[vmem] * 5,
        out_specs=[vmem] * 3,
        out_shape=[jax.ShapeDtypeStruct((rows, width), bf16), edge, edge],
        scratch_shapes=[
            pltpu.VMEM((rows, n3.shape[0] + f3.shape[0]), bf16),
            pltpu.VMEM((rows, width), f32),
        ],
        compiler_params=pltpu.CompilerParams(vmem_limit_bytes=12 * 2**20),
        name="decode_edges",
    )(total, o3, n3, f3, w_dec)


def main_kernel(hidden, dec_ref, main):
    edge = (dec_ref.shape[0] - main.shape[0]) // 2
    main[...] = lax.dot_general(
        dec_ref[pl.ds(edge, main.shape[0])],
        hidden[...],
        (((1,), (1,)), ((), ())),
        preferred_element_type=f32,
    )


def decode_main(hidden, w_dec):
    cells = w_dec.shape[0] // (PATCH + 2 * OV)
    vmem = pl.BlockSpec(memory_space=pltpu.VMEM)
    return pl.pallas_call(
        main_kernel,
        in_specs=[vmem] * 2,
        out_specs=vmem,
        out_shape=jax.ShapeDtypeStruct((PATCH * cells, hidden.shape[0]), f32),
        compiler_params=pltpu.CompilerParams(vmem_limit_bytes=8 * 2**20),
        name="decode_main",
    )(hidden, w_dec)


def join_kernel(main, inner, outer, field):
    _, core = place()
    edge = inner.shape[0]
    rest = main.shape[0] - edge
    before = jnp.where(core == 0, outer[...], inner[...]).astype(f32)
    after = jnp.where(core == 0, inner[...], outer[...]).astype(f32)
    field[:edge] = main[:edge] + before
    field[edge:rest] = main[edge:rest]
    field[rest:] = main[rest:] + after


def join(main, inner, outer):
    vmem = pl.BlockSpec(memory_space=pltpu.VMEM)
    return pl.pallas_call(
        join_kernel,
        in_specs=[vmem] * 3,
        out_specs=vmem,
        out_shape=jax.ShapeDtypeStruct(main.shape, f32),
        compiler_params=pltpu.CompilerParams(vmem_limit_bytes=4 * 2**20),
        name="join",
    )(main, inner, outer)


def gathered_kernel(*refs):
    rows = refs[0].shape[0]
    for i, part in enumerate(refs[:-1]):
        refs[-1][pl.ds(i * rows, rows)] = part[...]


def gathered(parts):
    rows, width = parts[0].shape
    vmem = pl.BlockSpec(memory_space=pltpu.VMEM)
    return pl.pallas_call(
        gathered_kernel,
        in_specs=[vmem] * len(parts),
        out_specs=vmem,
        out_shape=jax.ShapeDtypeStruct((len(parts) * rows, width), bf16),
        compiler_params=pltpu.CompilerParams(vmem_limit_bytes=4 * 2**20),
        name="gathered",
    )(*parts)


def first_way(value):
    count = lax.axis_size("ctx") * lax.axis_size("head")
    pairs = [(i, i ^ (1 if (i // 4) % 2 == 0 else 2)) for i in range(count)]
    return lax.ppermute(value, ("ctx", "head"), pairs)


def second_way(value):
    count = lax.axis_size("ctx") * lax.axis_size("head")
    pairs = [(i, i ^ (2 if (i // 4) % 2 == 0 else 1)) for i in range(count)]
    return lax.ppermute(value, ("ctx", "head"), pairs)


def fast_body(tokens, w_qkv, w_out, w_dec):
    rows = tokens.shape[0]

    w1 = first_way(w_out)

    p0, p1, p2, p3, p0_sent = project(tokens, w_qkv)
    r2, r3 = swapped(p2, "ctx", 4), swapped(p3, "ctx", 6)
    c0 = swapped(p0_sent, "ctx", 1)
    p1, c0 = lax.optimization_barrier((p1, c0))
    r1 = swapped(p1, "ctx", 2)
    c1, c2, c3 = (swapped(part, "ctx", 1) for part in (r1, r2, r3))
    w1, c1, c2, c3 = lax.optimization_barrier((w1, c1, c2, c3))
    size = w_out.shape[0] // 2
    half = lax.dynamic_slice_in_dim(w1, lax.rem(lax.axis_index("ctx"), 2) * size, size, 0)
    n3 = second_way(half)

    o2, o3 = attend([r2, r3, p0, r1, c0, c1, c2, c3])
    o0, o1 = attend([p0, r1, r2, r3, c0, c1, c2, c3])
    own = gathered([o0, swapped(o1, "ctx", 2), swapped(o2, "ctx", 4), swapped(o3, "ctx", 6)])
    own, w1, n3 = lax.optimization_barrier((own, w1, n3))
    a1, a2 = first_way(own), second_way(own)
    w2 = swapped(w1, "ctx", 1)
    a1, a2, n3 = lax.optimization_barrier((a1, a2, n3))
    a3 = second_way(a1)
    f3 = swapped(n3, "ctx", 1)
    total = mix(tokens, [own, a1, a2], [w_out, w1, w2])

    dec = w_dec.transpose(1, 2, 0)
    dec = dec.reshape(-1, dec.shape[2])
    hidden, inner, outer = decode_edges(total, a3, n3, f3, dec)
    count = lax.axis_size("ctx")
    pairs = [(i, (i - 1 + 2 * (i % 2)) % count) for i in range(count)]
    outer = lax.ppermute(outer, "ctx", pairs)
    inner = swapped(inner, "ctx", 1)
    field = join(decode_main(hidden, dec), inner, outer)
    return field.reshape(PATCH, -1, rows).transpose(2, 0, 1)


def general_body(tokens, w_qkv, w_out, w_dec):
    rows = tokens.shape[0]
    local_heads = w_qkv.shape[2] // HD
    xf = tokens.astype(f32)
    normed = rms_scale(xf).astype(bf16)
    projected = jnp.einsum("td,kdc->ktc", normed, w_qkv, preferred_element_type=f32).astype(bf16)
    queries = projected[0].reshape(rows, local_heads, HD)
    keyvals = projected[1:]
    scale = HD ** (-0.5)

    def block_update(carry, block):
        best, total, accum = carry
        keys = block[0].reshape(-1, local_heads, HD)
        values = block[1].reshape(-1, local_heads, HD)
        scores = jnp.einsum("thd,rhd->thr", queries, keys, preferred_element_type=f32) * scale
        fresh = jnp.maximum(best, jnp.max(scores, axis=-1))
        shrink = jnp.exp(best - fresh)
        weights = jnp.exp(scores - fresh[..., None])
        total = total * shrink + jnp.sum(weights, axis=-1)
        accum = accum * shrink[..., None] + jnp.einsum(
            "thr,rhd->thd", weights.astype(bf16), values, preferred_element_type=f32
        )
        return (fresh, total, accum)

    initial = (
        jnp.full((rows, local_heads), -1e30, f32),
        jnp.zeros((rows, local_heads), f32),
        jnp.zeros((rows, local_heads, HD), f32),
    )
    piece = lax.all_gather(keyvals, "ctx", axis=1, tiled=True)
    length = piece.shape[1]
    span = math.gcd(length, 1024)

    def one_block(index, inner):
        block = lax.dynamic_slice_in_dim(piece, index * span, span, 1)
        return block_update(inner, block)

    best, total, accum = lax.fori_loop(0, length // span, one_block, initial)
    attended = (accum / total[..., None]).astype(bf16).reshape(rows, local_heads * HD)
    partial_out = jnp.dot(attended, w_out, preferred_element_type=f32)
    mixed = lax.psum(partial_out.astype(bf16), "head").astype(f32)
    hidden = rms_scale(xf + mixed).astype(bf16)
    extended = jnp.dot(hidden, w_dec.reshape(w_dec.shape[0], -1), preferred_element_type=f32)
    extended = extended.reshape(rows, w_dec.shape[1], w_dec.shape[2])
    from_before = passed_along(extended[:, PATCH + OV :].astype(bf16), "ctx", 1).astype(f32)
    from_after = passed_along(extended[:, :OV].astype(bf16), "ctx", -1).astype(f32)
    middle = extended[:, OV : OV + PATCH]
    return jnp.concatenate(
        [
            middle[:, :OV] + from_before,
            middle[:, OV : PATCH - OV],
            middle[:, PATCH - OV :] + from_after,
        ],
        axis=1,
    )


def body(tokens, w_qkv, w_out, w_dec):
    fits = lax.axis_size("ctx") == 8 and lax.axis_size("head") == 4
    fits = fits and w_qkv.shape[2] == 4 * LANES and tokens.shape[0] % 256 == 0
    run = fast_body if fits else general_body
    return run(tokens, w_qkv, w_out, w_dec)


def solution(mesh):
    return jax.shard_map(
        body,
        mesh=mesh,
        in_specs=(P("ctx", None), P(None, None, "head"), P("head", None), P(None, None, "head")),
        out_specs=P("ctx", None, "head"),
        check_vma=False,
    )
```

```python
import functools
import math

import jax
import jax.numpy as jnp
from jax import lax
from jax.experimental import pallas as pl
from jax.experimental.pallas import tpu as pltpu
from jax.sharding import PartitionSpec as P

HD = 64
PATCH = 8
OV = 2
LANES = 128

eps = 1e-05
bf16 = jnp.bfloat16
f32 = jnp.float32


def passed_along(value, axis, steps):
    count = lax.axis_size(axis)
    pairs = [(source, (source + steps) % count) for source in range(count)]
    return lax.ppermute(value, axis, pairs)


def swapped(value, axis, bits):
    count = lax.axis_size(axis)
    return lax.ppermute(value, axis, [(i, i ^ bits) for i in range(count)])


def rms_scale(values):
    return values * lax.rsqrt(jnp.mean(values * values, axis=-1, keepdims=True) + eps)


def place():
    ctx = lax.axis_index("ctx")
    return lax.div(ctx, 2), lax.rem(ctx, 2)


def project_kernel(x_hbm, w_hbm, *refs):
    packs = refs[:4]
    x_ref, w_ref, x_sem, w_sem = refs[4:]
    z, _ = place()
    rows = x_ref.shape[0]
    x_copy = pltpu.make_async_copy(x_hbm, x_ref, x_sem)
    x_copy.start()
    copies = [pltpu.make_async_copy(w_hbm.at[k], w_ref.at[k], w_sem.at[k]) for k in range(3)]
    for copy in copies:
        copy.start()
    x_copy.wait()
    x = x_ref[...].astype(f32)
    scale = lax.rsqrt(jnp.mean(x * x, axis=-1, keepdims=True) + eps)
    q_scale = scale * (HD ** (-0.5) * math.log2(math.e))
    odd = lax.rem(z, 2) == 1
    upper = lax.div(z, 2) == 1
    for k, copy in enumerate(copies):
        copy.wait()
        out = jnp.dot(x_ref[...], w_ref[k], preferred_element_type=f32)
        out = (out * (q_scale if k == 0 else scale)).astype(bf16)
        parts = [out[:, i * LANES : (i + 1) * LANES] for i in range(4)]
        parts = [jnp.where(odd, parts[i ^ 1], parts[i]) for i in range(4)]
        parts = [jnp.where(upper, parts[i ^ 2], parts[i]) for i in range(4)]
        for pack, part in zip(packs, parts):
            pack[pl.ds(k * rows, rows)] = part


def project(tokens, w_qkv):
    rows, width = tokens.shape
    hbm = pl.BlockSpec(memory_space=pltpu.HBM)
    vmem = pl.BlockSpec(memory_space=pltpu.VMEM)
    return pl.pallas_call(
        project_kernel,
        in_specs=[hbm] * 2,
        out_specs=[vmem] * 4,
        out_shape=[jax.ShapeDtypeStruct((3 * rows, LANES), bf16)] * 4,
        scratch_shapes=[
            pltpu.VMEM((rows, width), bf16),
            pltpu.VMEM(w_qkv.shape, bf16),
            pltpu.SemaphoreType.DMA(()),
            pltpu.SemaphoreType.DMA((3,)),
        ],
        compiler_params=pltpu.CompilerParams(vmem_limit_bytes=53 * 2**20),
        name="project",
    )(tokens, w_qkv)


def attention_kernel(*refs):
    packs, outs = refs[:8], refs[8:10]
    k_all, v_lo, v_hi, q_all = refs[10:]
    rows = packs[0].shape[0] // 3
    low = lax.broadcasted_iota(jnp.int32, (1, LANES), 1) < HD
    one = jnp.ones((), bf16)
    zero = jnp.zeros((), bf16)
    for i, pack in enumerate(packs):
        part = pl.ds(i * rows, rows)
        k_all[part] = pack[rows : 2 * rows]
        v = pack[2 * rows :]
        v_lo[part] = jnp.where(low, v, one)
        v_hi[part] = jnp.where(low, one, v)
    for i in range(2):
        q_all[pl.ds(i * rows, rows)] = packs[i][:rows]

    def score(q):
        return lax.dot_general(
            q, k_all[...], (((1,), (1,)), ((), ())), preferred_element_type=f32
        )

    def weigh(scores):
        return jnp.exp2(scores - jnp.max(scores, axis=-1, keepdims=True)).astype(bf16)

    q = q_all[...]
    lo_scores = score(jnp.where(low, q, zero))
    hi_scores = score(jnp.where(low, zero, q))
    lo_weights, hi_weights = weigh(lo_scores), weigh(hi_scores)
    lo = jnp.dot(lo_weights, v_lo[...], preferred_element_type=f32)
    hi = jnp.dot(hi_weights, v_hi[...], preferred_element_type=f32)
    top = jnp.where(low, lo, hi)
    bottom = pltpu.roll(jnp.where(low, hi, lo), HD, 1)
    attended = (top / bottom).astype(bf16)
    for i in range(2):
        outs[i][...] = attended[i * rows : (i + 1) * rows]


def attend(packs):
    rows = packs[0].shape[0] // 3
    keys = rows * len(packs)
    vmem = pl.BlockSpec(memory_space=pltpu.VMEM)
    return pl.pallas_call(
        attention_kernel,
        in_specs=[vmem] * len(packs),
        out_specs=[vmem] * 2,
        out_shape=[jax.ShapeDtypeStruct((rows, LANES), bf16)] * 2,
        scratch_shapes=[pltpu.VMEM((keys, LANES), bf16)] * 3 + [pltpu.VMEM((2 * rows, LANES), bf16)],
        compiler_params=pltpu.CompilerParams(vmem_limit_bytes=24 * 2**20),
        name="attend",
    )(*packs)


def mix_kernel(x_ref, o0, o1, o2, own, w1, w2, total, att):
    z, _ = place()
    rows, width = x_ref.shape
    local = own.shape[0]
    for s in range(4):
        for i, o in enumerate((o0, o1, o2)):
            at = pl.multiple_of(i * local + (z ^ s) * LANES, LANES)
            att[:, pl.ds(at, LANES)] = o[pl.ds(s * rows, rows)]
    step = 512
    for n in range(0, width, step):
        w = jnp.concatenate([part[:, n : n + step] for part in (own, w1, w2)], axis=0)
        mixed = jnp.dot(att[...], w, preferred_element_type=f32)
        total[:, n : n + step] = x_ref[:, n : n + step].astype(f32) + mixed


def mix(tokens, outs, parts):
    rows, width = tokens.shape
    vmem = pl.BlockSpec(memory_space=pltpu.VMEM)
    return pl.pallas_call(
        mix_kernel,
        in_specs=[vmem] * 7,
        out_specs=vmem,
        out_shape=jax.ShapeDtypeStruct((rows, width), f32),
        scratch_shapes=[pltpu.VMEM((rows, 3 * parts[0].shape[0]), bf16)],
        compiler_params=pltpu.CompilerParams(vmem_limit_bytes=12 * 2**20),
        name="mix",
    )(tokens, *outs, *parts)


def edges_kernel(total, o3, n3, f3, dec_ref, hidden, inner, outer, att, held):
    z, core = place()
    rows, width = total.shape
    for s in range(4):
        spot = z ^ s ^ (2 * core)
        att[:, pl.ds(pl.multiple_of(spot * LANES, LANES), LANES)] = o3[pl.ds(s * rows, rows)]
    step = 512
    squares = jnp.zeros((rows, LANES), f32)
    for n in range(0, width, step):
        w = jnp.concatenate([part[:, n : n + step] for part in (n3, f3)], axis=0)
        mixed = total[:, n : n + step] + jnp.dot(att[...], w, preferred_element_type=f32)
        held[:, n : n + step] = mixed
        for i in range(0, step, LANES):
            squares += mixed[:, i : i + LANES] * mixed[:, i : i + LANES]
    scale = lax.rsqrt(jnp.sum(squares, axis=-1, keepdims=True) * (1.0 / width) + eps)
    hidden[...] = (held[...] * scale).astype(bf16)
    edge = inner.shape[0]
    last = dec_ref.shape[0] - edge

    def cells(part):
        return lax.dot_general(
            dec_ref[part], hidden[...], (((1,), (1,)), ((), ())), preferred_element_type=f32
        ).astype(bf16)

    down = cells(pl.ds(0, edge))
    up = cells(pl.ds(last, edge))
    inner[...] = jnp.where(core == 0, up, down)
    outer[...] = jnp.where(core == 0, down, up)


def decode_edges(total, o3, n3, f3, w_dec):
    rows, width = total.shape
    cells = w_dec.shape[0] // (PATCH + 2 * OV)
    vmem = pl.BlockSpec(memory_space=pltpu.VMEM)
    edge = jax.ShapeDtypeStruct((OV * cells, rows), bf16)
    return pl.pallas_call(
        edges_kernel,
        in_specs=[vmem] * 5,
        out_specs=[vmem] * 3,
        out_shape=[jax.ShapeDtypeStruct((rows, width), bf16), edge, edge],
        scratch_shapes=[
            pltpu.VMEM((rows, n3.shape[0] + f3.shape[0]), bf16),
            pltpu.VMEM((rows, width), f32),
        ],
        compiler_params=pltpu.CompilerParams(vmem_limit_bytes=12 * 2**20),
        name="decode_edges",
    )(total, o3, n3, f3, w_dec)


def main_kernel(hidden, dec_ref, main):
    edge = (dec_ref.shape[0] - main.shape[0]) // 2
    main[...] = lax.dot_general(
        dec_ref[pl.ds(edge, main.shape[0])],
        hidden[...],
        (((1,), (1,)), ((), ())),
        preferred_element_type=f32,
    )


def decode_main(hidden, w_dec):
    cells = w_dec.shape[0] // (PATCH + 2 * OV)
    vmem = pl.BlockSpec(memory_space=pltpu.VMEM)
    return pl.pallas_call(
        main_kernel,
        in_specs=[vmem] * 2,
        out_specs=vmem,
        out_shape=jax.ShapeDtypeStruct((PATCH * cells, hidden.shape[0]), f32),
        compiler_params=pltpu.CompilerParams(vmem_limit_bytes=8 * 2**20),
        name="decode_main",
    )(hidden, w_dec)


def join_kernel(main, inner, outer, field):
    _, core = place()
    edge = inner.shape[0]
    rest = main.shape[0] - edge
    before = jnp.where(core == 0, outer[...], inner[...]).astype(f32)
    after = jnp.where(core == 0, inner[...], outer[...]).astype(f32)
    field[:edge] = main[:edge] + before
    field[edge:rest] = main[edge:rest]
    field[rest:] = main[rest:] + after


def join(main, inner, outer):
    vmem = pl.BlockSpec(memory_space=pltpu.VMEM)
    return pl.pallas_call(
        join_kernel,
        in_specs=[vmem] * 3,
        out_specs=vmem,
        out_shape=jax.ShapeDtypeStruct(main.shape, f32),
        compiler_params=pltpu.CompilerParams(vmem_limit_bytes=4 * 2**20),
        name="join",
    )(main, inner, outer)


def gathered_kernel(*refs):
    rows = refs[0].shape[0]
    for i, part in enumerate(refs[:-1]):
        refs[-1][pl.ds(i * rows, rows)] = part[...]


def gathered(parts):
    rows, width = parts[0].shape
    vmem = pl.BlockSpec(memory_space=pltpu.VMEM)
    return pl.pallas_call(
        gathered_kernel,
        in_specs=[vmem] * len(parts),
        out_specs=vmem,
        out_shape=jax.ShapeDtypeStruct((len(parts) * rows, width), bf16),
        compiler_params=pltpu.CompilerParams(vmem_limit_bytes=4 * 2**20),
        name="gathered",
    )(*parts)


def first_way(value):
    count = lax.axis_size("ctx") * lax.axis_size("head")
    pairs = [(i, i ^ (1 if (i // 4) % 2 == 0 else 2)) for i in range(count)]
    return lax.ppermute(value, ("ctx", "head"), pairs)


def second_way(value):
    count = lax.axis_size("ctx") * lax.axis_size("head")
    pairs = [(i, i ^ (2 if (i // 4) % 2 == 0 else 1)) for i in range(count)]
    return lax.ppermute(value, ("ctx", "head"), pairs)


def fast_body(tokens, w_qkv, w_out, w_dec):
    rows = tokens.shape[0]

    w1 = first_way(w_out)

    p0, p1, p2, p3 = project(tokens, w_qkv)
    r2, r3 = swapped(p2, "ctx", 4), swapped(p3, "ctx", 6)
    c0 = swapped(p0, "ctx", 1)
    p1, c0 = lax.optimization_barrier((p1, c0))
    r1 = swapped(p1, "ctx", 2)
    c1, c2, c3 = (swapped(part, "ctx", 1) for part in (r1, r2, r3))
    w1, c1, c2, c3 = lax.optimization_barrier((w1, c1, c2, c3))
    size = w_out.shape[0] // 2
    half = lax.dynamic_slice_in_dim(w1, lax.rem(lax.axis_index("ctx"), 2) * size, size, 0)
    n3 = second_way(half)

    o2, o3 = attend([r2, r3, p0, r1, c0, c1, c2, c3])
    o0, o1 = attend([p0, r1, r2, r3, c0, c1, c2, c3])
    own = gathered([o0, swapped(o1, "ctx", 2), swapped(o2, "ctx", 4), swapped(o3, "ctx", 6)])
    own, n3 = lax.optimization_barrier((own, n3))
    a1, a2 = first_way(own), second_way(own)
    w2 = swapped(w1, "ctx", 1)
    a1, a2, n3 = lax.optimization_barrier((a1, a2, n3))
    a3 = second_way(a1)
    f3 = swapped(n3, "ctx", 1)
    total = mix(tokens, [own, a1, a2], [w_out, w1, w2])

    dec = w_dec.transpose(1, 2, 0)
    dec = dec.reshape(-1, dec.shape[2])
    hidden, inner, outer = decode_edges(total, a3, n3, f3, dec)
    count = lax.axis_size("ctx")
    pairs = [(i, (i - 1 + 2 * (i % 2)) % count) for i in range(count)]
    outer = lax.ppermute(outer, "ctx", pairs)
    inner = swapped(inner, "ctx", 1)
    field = join(decode_main(hidden, dec), inner, outer)
    return field.reshape(PATCH, -1, rows).transpose(2, 0, 1)


def general_body(tokens, w_qkv, w_out, w_dec):
    rows = tokens.shape[0]
    local_heads = w_qkv.shape[2] // HD
    xf = tokens.astype(f32)
    normed = rms_scale(xf).astype(bf16)
    projected = jnp.einsum("td,kdc->ktc", normed, w_qkv, preferred_element_type=f32).astype(bf16)
    queries = projected[0].reshape(rows, local_heads, HD)
    keyvals = projected[1:]
    scale = HD ** (-0.5)

    def block_update(carry, block):
        best, total, accum = carry
        keys = block[0].reshape(-1, local_heads, HD)
        values = block[1].reshape(-1, local_heads, HD)
        scores = jnp.einsum("thd,rhd->thr", queries, keys, preferred_element_type=f32) * scale
        fresh = jnp.maximum(best, jnp.max(scores, axis=-1))
        shrink = jnp.exp(best - fresh)
        weights = jnp.exp(scores - fresh[..., None])
        total = total * shrink + jnp.sum(weights, axis=-1)
        accum = accum * shrink[..., None] + jnp.einsum(
            "thr,rhd->thd", weights.astype(bf16), values, preferred_element_type=f32
        )
        return (fresh, total, accum)

    initial = (
        jnp.full((rows, local_heads), -1e30, f32),
        jnp.zeros((rows, local_heads), f32),
        jnp.zeros((rows, local_heads, HD), f32),
    )
    piece = lax.all_gather(keyvals, "ctx", axis=1, tiled=True)
    length = piece.shape[1]
    span = math.gcd(length, 1024)

    def one_block(index, inner):
        block = lax.dynamic_slice_in_dim(piece, index * span, span, 1)
        return block_update(inner, block)

    best, total, accum = lax.fori_loop(0, length // span, one_block, initial)
    attended = (accum / total[..., None]).astype(bf16).reshape(rows, local_heads * HD)
    partial_out = jnp.dot(attended, w_out, preferred_element_type=f32)
    mixed = lax.psum(partial_out.astype(bf16), "head").astype(f32)
    hidden = rms_scale(xf + mixed).astype(bf16)
    extended = jnp.dot(hidden, w_dec.reshape(w_dec.shape[0], -1), preferred_element_type=f32)
    extended = extended.reshape(rows, w_dec.shape[1], w_dec.shape[2])
    from_before = passed_along(extended[:, PATCH + OV :].astype(bf16), "ctx", 1).astype(f32)
    from_after = passed_along(extended[:, :OV].astype(bf16), "ctx", -1).astype(f32)
    middle = extended[:, OV : OV + PATCH]
    return jnp.concatenate(
        [
            middle[:, :OV] + from_before,
            middle[:, OV : PATCH - OV],
            middle[:, PATCH - OV :] + from_after,
        ],
        axis=1,
    )


def body(tokens, w_qkv, w_out, w_dec):
    fits = lax.axis_size("ctx") == 8 and lax.axis_size("head") == 4
    fits = fits and w_qkv.shape[2] == 4 * LANES and tokens.shape[0] % 256 == 0
    run = fast_body if fits else general_body
    return run(tokens, w_qkv, w_out, w_dec)


def solution(mesh):
    return jax.shard_map(
        body,
        mesh=mesh,
        in_specs=(P("ctx", None), P(None, None, "head"), P("head", None), P(None, None, "head")),
        out_specs=P("ctx", None, "head"),
        check_vma=False,
    )
```

```python
import functools
import math

import jax
import jax.numpy as jnp
from jax import lax
from jax.experimental import pallas as pl
from jax.experimental.pallas import tpu as pltpu
from jax.sharding import PartitionSpec as P

HD = 64
PATCH = 8
OV = 2
LANES = 128

eps = 1e-05
bf16 = jnp.bfloat16
f32 = jnp.float32


def passed_along(value, axis, steps):
    count = lax.axis_size(axis)
    pairs = [(source, (source + steps) % count) for source in range(count)]
    return lax.ppermute(value, axis, pairs)


def swapped(value, axis, bits):
    count = lax.axis_size(axis)
    return lax.ppermute(value, axis, [(i, i ^ bits) for i in range(count)])


def rms_scale(values):
    return values * lax.rsqrt(jnp.mean(values * values, axis=-1, keepdims=True) + eps)


def place():
    ctx = lax.axis_index("ctx")
    return lax.div(ctx, 2), lax.rem(ctx, 2)


def project_kernel(x_hbm, w_hbm, *refs):
    packs = refs[:4]
    x_ref, w_ref, x_sem, w_sem = refs[4:]
    z, _ = place()
    rows = x_ref.shape[0]
    x_copy = pltpu.make_async_copy(x_hbm, x_ref, x_sem)
    x_copy.start()
    copies = [pltpu.make_async_copy(w_hbm.at[k], w_ref.at[k], w_sem.at[k]) for k in range(3)]
    copies[0].start()
    x_copy.wait()
    copies[1].start()
    copies[2].start()
    x = x_ref[...].astype(f32)
    scale = lax.rsqrt(jnp.mean(x * x, axis=-1, keepdims=True) + eps)
    q_scale = scale * (HD ** (-0.5) * math.log2(math.e))
    odd = lax.rem(z, 2) == 1
    upper = lax.div(z, 2) == 1
    for k, copy in enumerate(copies):
        copy.wait()
        out = jnp.dot(x_ref[...], w_ref[k], preferred_element_type=f32)
        out = (out * (q_scale if k == 0 else scale)).astype(bf16)
        parts = [out[:, i * LANES : (i + 1) * LANES] for i in range(4)]
        parts = [jnp.where(odd, parts[i ^ 1], parts[i]) for i in range(4)]
        parts = [jnp.where(upper, parts[i ^ 2], parts[i]) for i in range(4)]
        for pack, part in zip(packs, parts):
            pack[pl.ds(k * rows, rows)] = part


def project(tokens, w_qkv):
    rows, width = tokens.shape
    hbm = pl.BlockSpec(memory_space=pltpu.HBM)
    vmem = pl.BlockSpec(memory_space=pltpu.VMEM)
    return pl.pallas_call(
        project_kernel,
        in_specs=[hbm] * 2,
        out_specs=[vmem] * 4,
        out_shape=[jax.ShapeDtypeStruct((3 * rows, LANES), bf16)] * 4,
        scratch_shapes=[
            pltpu.VMEM((rows, width), bf16),
            pltpu.VMEM(w_qkv.shape, bf16),
            pltpu.SemaphoreType.DMA(()),
            pltpu.SemaphoreType.DMA((3,)),
        ],
        compiler_params=pltpu.CompilerParams(vmem_limit_bytes=53 * 2**20),
        name="project",
    )(tokens, w_qkv)


def attention_kernel(*refs):
    packs, outs = refs[:8], refs[8:10]
    k_all, v_lo, v_hi, q_all = refs[10:]
    rows = packs[0].shape[0] // 3
    low = lax.broadcasted_iota(jnp.int32, (1, LANES), 1) < HD
    one = jnp.ones((), bf16)
    zero = jnp.zeros((), bf16)
    for i, pack in enumerate(packs):
        part = pl.ds(i * rows, rows)
        k_all[part] = pack[rows : 2 * rows]
        v = pack[2 * rows :]
        v_lo[part] = jnp.where(low, v, one)
        v_hi[part] = jnp.where(low, one, v)
    for i in range(2):
        q_all[pl.ds(i * rows, rows)] = packs[i][:rows]

    def score(q):
        return lax.dot_general(
            q, k_all[...], (((1,), (1,)), ((), ())), preferred_element_type=f32
        )

    def weigh(scores):
        return jnp.exp2(scores - jnp.max(scores, axis=-1, keepdims=True)).astype(bf16)

    q = q_all[...]
    lo_scores = score(jnp.where(low, q, zero))
    hi_scores = score(jnp.where(low, zero, q))
    lo_weights, hi_weights = weigh(lo_scores), weigh(hi_scores)
    lo = jnp.dot(lo_weights, v_lo[...], preferred_element_type=f32)
    hi = jnp.dot(hi_weights, v_hi[...], preferred_element_type=f32)
    top = jnp.where(low, lo, hi)
    bottom = pltpu.roll(jnp.where(low, hi, lo), HD, 1)
    attended = (top / bottom).astype(bf16)
    for i in range(2):
        outs[i][...] = attended[i * rows : (i + 1) * rows]


def attend(packs):
    rows = packs[0].shape[0] // 3
    keys = rows * len(packs)
    vmem = pl.BlockSpec(memory_space=pltpu.VMEM)
    return pl.pallas_call(
        attention_kernel,
        in_specs=[vmem] * len(packs),
        out_specs=[vmem] * 2,
        out_shape=[jax.ShapeDtypeStruct((rows, LANES), bf16)] * 2,
        scratch_shapes=[pltpu.VMEM((keys, LANES), bf16)] * 3 + [pltpu.VMEM((2 * rows, LANES), bf16)],
        compiler_params=pltpu.CompilerParams(vmem_limit_bytes=24 * 2**20),
        name="attend",
    )(*packs)


def mix_kernel(x_ref, o0, o1, o2, own, w1, w2, total, att):
    z, _ = place()
    rows, width = x_ref.shape
    local = own.shape[0]
    for s in range(4):
        for i, o in enumerate((o0, o1, o2)):
            at = pl.multiple_of(i * local + (z ^ s) * LANES, LANES)
            att[:, pl.ds(at, LANES)] = o[pl.ds(s * rows, rows)]
    step = 512
    for n in range(0, width, step):
        w = jnp.concatenate([part[:, n : n + step] for part in (own, w1, w2)], axis=0)
        mixed = jnp.dot(att[...], w, preferred_element_type=f32)
        total[:, n : n + step] = x_ref[:, n : n + step].astype(f32) + mixed


def mix(tokens, outs, parts):
    rows, width = tokens.shape
    vmem = pl.BlockSpec(memory_space=pltpu.VMEM)
    return pl.pallas_call(
        mix_kernel,
        in_specs=[vmem] * 7,
        out_specs=vmem,
        out_shape=jax.ShapeDtypeStruct((rows, width), f32),
        scratch_shapes=[pltpu.VMEM((rows, 3 * parts[0].shape[0]), bf16)],
        compiler_params=pltpu.CompilerParams(vmem_limit_bytes=12 * 2**20),
        name="mix",
    )(tokens, *outs, *parts)


def edges_kernel(total, o3, n3, f3, dec_ref, hidden, inner, outer, att, held):
    z, core = place()
    rows, width = total.shape
    for s in range(4):
        spot = z ^ s ^ (2 * core)
        att[:, pl.ds(pl.multiple_of(spot * LANES, LANES), LANES)] = o3[pl.ds(s * rows, rows)]
    step = 512
    squares = jnp.zeros((rows, LANES), f32)
    for n in range(0, width, step):
        w = jnp.concatenate([part[:, n : n + step] for part in (n3, f3)], axis=0)
        mixed = total[:, n : n + step] + jnp.dot(att[...], w, preferred_element_type=f32)
        held[:, n : n + step] = mixed
        for i in range(0, step, LANES):
            squares += mixed[:, i : i + LANES] * mixed[:, i : i + LANES]
    scale = lax.rsqrt(jnp.sum(squares, axis=-1, keepdims=True) * (1.0 / width) + eps)
    hidden[...] = (held[...] * scale).astype(bf16)
    edge = inner.shape[0]
    last = dec_ref.shape[0] - edge

    def cells(part):
        return lax.dot_general(
            dec_ref[part], hidden[...], (((1,), (1,)), ((), ())), preferred_element_type=f32
        ).astype(bf16)

    down = cells(pl.ds(0, edge))
    up = cells(pl.ds(last, edge))
    inner[...] = jnp.where(core == 0, up, down)
    outer[...] = jnp.where(core == 0, down, up)


def decode_edges(total, o3, n3, f3, w_dec):
    rows, width = total.shape
    cells = w_dec.shape[0] // (PATCH + 2 * OV)
    vmem = pl.BlockSpec(memory_space=pltpu.VMEM)
    edge = jax.ShapeDtypeStruct((OV * cells, rows), bf16)
    return pl.pallas_call(
        edges_kernel,
        in_specs=[vmem] * 5,
        out_specs=[vmem] * 3,
        out_shape=[jax.ShapeDtypeStruct((rows, width), bf16), edge, edge],
        scratch_shapes=[
            pltpu.VMEM((rows, n3.shape[0] + f3.shape[0]), bf16),
            pltpu.VMEM((rows, width), f32),
        ],
        compiler_params=pltpu.CompilerParams(vmem_limit_bytes=12 * 2**20),
        name="decode_edges",
    )(total, o3, n3, f3, w_dec)


def main_kernel(hidden, dec_ref, main):
    edge = (dec_ref.shape[0] - main.shape[0]) // 2
    main[...] = lax.dot_general(
        dec_ref[pl.ds(edge, main.shape[0])],
        hidden[...],
        (((1,), (1,)), ((), ())),
        preferred_element_type=f32,
    )


def decode_main(hidden, w_dec):
    cells = w_dec.shape[0] // (PATCH + 2 * OV)
    vmem = pl.BlockSpec(memory_space=pltpu.VMEM)
    return pl.pallas_call(
        main_kernel,
        in_specs=[vmem] * 2,
        out_specs=vmem,
        out_shape=jax.ShapeDtypeStruct((PATCH * cells, hidden.shape[0]), f32),
        compiler_params=pltpu.CompilerParams(vmem_limit_bytes=8 * 2**20),
        name="decode_main",
    )(hidden, w_dec)


def join_kernel(main, inner, outer, field):
    _, core = place()
    edge = inner.shape[0]
    rest = main.shape[0] - edge
    before = jnp.where(core == 0, outer[...], inner[...]).astype(f32)
    after = jnp.where(core == 0, inner[...], outer[...]).astype(f32)
    field[:edge] = main[:edge] + before
    field[edge:rest] = main[edge:rest]
    field[rest:] = main[rest:] + after


def join(main, inner, outer):
    vmem = pl.BlockSpec(memory_space=pltpu.VMEM)
    return pl.pallas_call(
        join_kernel,
        in_specs=[vmem] * 3,
        out_specs=vmem,
        out_shape=jax.ShapeDtypeStruct(main.shape, f32),
        compiler_params=pltpu.CompilerParams(vmem_limit_bytes=4 * 2**20),
        name="join",
    )(main, inner, outer)


def gathered_kernel(*refs):
    rows = refs[0].shape[0]
    for i, part in enumerate(refs[:-1]):
        refs[-1][pl.ds(i * rows, rows)] = part[...]


def gathered(parts):
    rows, width = parts[0].shape
    vmem = pl.BlockSpec(memory_space=pltpu.VMEM)
    return pl.pallas_call(
        gathered_kernel,
        in_specs=[vmem] * len(parts),
        out_specs=vmem,
        out_shape=jax.ShapeDtypeStruct((len(parts) * rows, width), bf16),
        compiler_params=pltpu.CompilerParams(vmem_limit_bytes=4 * 2**20),
        name="gathered",
    )(*parts)


def halved_kernel(block, half):
    _, core = place()
    rows = half.shape[0]
    half[...] = block[pl.ds(pl.multiple_of(core * rows, rows), rows)]


def halved(block):
    rows, width = block.shape
    vmem = pl.BlockSpec(memory_space=pltpu.VMEM)
    return pl.pallas_call(
        halved_kernel,
        in_specs=[vmem],
        out_specs=vmem,
        out_shape=jax.ShapeDtypeStruct((rows // 2, width), bf16),
        compiler_params=pltpu.CompilerParams(vmem_limit_bytes=4 * 2**20),
        name="halved",
    )(block)


def first_way(value):
    count = lax.axis_size("ctx") * lax.axis_size("head")
    pairs = [(i, i ^ (1 if (i // 4) % 2 == 0 else 2)) for i in range(count)]
    return lax.ppermute(value, ("ctx", "head"), pairs)


def second_way(value):
    count = lax.axis_size("ctx") * lax.axis_size("head")
    pairs = [(i, i ^ (2 if (i // 4) % 2 == 0 else 1)) for i in range(count)]
    return lax.ppermute(value, ("ctx", "head"), pairs)


def fast_body(tokens, w_qkv, w_out, w_dec):
    rows = tokens.shape[0]

    w1 = first_way(w_out)

    p0, p1, p2, p3 = project(tokens, w_qkv)
    r2, r3 = swapped(p2, "ctx", 4), swapped(p3, "ctx", 6)
    c0 = swapped(p0, "ctx", 1)
    p1, c0 = lax.optimization_barrier((p1, c0))
    r1 = swapped(p1, "ctx", 2)
    c1, c2, c3 = (swapped(part, "ctx", 1) for part in (r1, r2, r3))
    w1, c1, c2, c3 = lax.optimization_barrier((w1, c1, c2, c3))
    n3 = second_way(halved(w1))

    o2, o3 = attend([r2, r3, p0, r1, c0, c1, c2, c3])
    w1, o2, o3 = lax.optimization_barrier((w1, o2, o3))
    w2 = swapped(w1, "ctx", 1)
    o0, o1 = attend([p0, r1, r2, r3, c0, c1, c2, c3])
    own = gathered([o0, swapped(o1, "ctx", 2), swapped(o2, "ctx", 4), swapped(o3, "ctx", 6)])
    own, n3 = lax.optimization_barrier((own, n3))
    a1, a2 = first_way(own), second_way(own)
    a1, a2, n3 = lax.optimization_barrier((a1, a2, n3))
    a3 = second_way(a1)
    f3 = swapped(n3, "ctx", 1)
    total = mix(tokens, [own, a1, a2], [w_out, w1, w2])

    dec = w_dec.transpose(1, 2, 0)
    dec = dec.reshape(-1, dec.shape[2])
    hidden, inner, outer = decode_edges(total, a3, n3, f3, dec)
    count = lax.axis_size("ctx")
    pairs = [(i, (i - 1 + 2 * (i % 2)) % count) for i in range(count)]
    outer = lax.ppermute(outer, "ctx", pairs)
    inner = swapped(inner, "ctx", 1)
    field = join(decode_main(hidden, dec), inner, outer)
    return field.reshape(PATCH, -1, rows).transpose(2, 0, 1)


def general_body(tokens, w_qkv, w_out, w_dec):
    rows = tokens.shape[0]
    local_heads = w_qkv.shape[2] // HD
    xf = tokens.astype(f32)
    normed = rms_scale(xf).astype(bf16)
    projected = jnp.einsum("td,kdc->ktc", normed, w_qkv, preferred_element_type=f32).astype(bf16)
    queries = projected[0].reshape(rows, local_heads, HD)
    keyvals = projected[1:]
    scale = HD ** (-0.5)

    def block_update(carry, block):
        best, total, accum = carry
        keys = block[0].reshape(-1, local_heads, HD)
        values = block[1].reshape(-1, local_heads, HD)
        scores = jnp.einsum("thd,rhd->thr", queries, keys, preferred_element_type=f32) * scale
        fresh = jnp.maximum(best, jnp.max(scores, axis=-1))
        shrink = jnp.exp(best - fresh)
        weights = jnp.exp(scores - fresh[..., None])
        total = total * shrink + jnp.sum(weights, axis=-1)
        accum = accum * shrink[..., None] + jnp.einsum(
            "thr,rhd->thd", weights.astype(bf16), values, preferred_element_type=f32
        )
        return (fresh, total, accum)

    initial = (
        jnp.full((rows, local_heads), -1e30, f32),
        jnp.zeros((rows, local_heads), f32),
        jnp.zeros((rows, local_heads, HD), f32),
    )
    piece = lax.all_gather(keyvals, "ctx", axis=1, tiled=True)
    length = piece.shape[1]
    span = math.gcd(length, 1024)

    def one_block(index, inner):
        block = lax.dynamic_slice_in_dim(piece, index * span, span, 1)
        return block_update(inner, block)

    best, total, accum = lax.fori_loop(0, length // span, one_block, initial)
    attended = (accum / total[..., None]).astype(bf16).reshape(rows, local_heads * HD)
    partial_out = jnp.dot(attended, w_out, preferred_element_type=f32)
    mixed = lax.psum(partial_out.astype(bf16), "head").astype(f32)
    hidden = rms_scale(xf + mixed).astype(bf16)
    extended = jnp.dot(hidden, w_dec.reshape(w_dec.shape[0], -1), preferred_element_type=f32)
    extended = extended.reshape(rows, w_dec.shape[1], w_dec.shape[2])
    from_before = passed_along(extended[:, PATCH + OV :].astype(bf16), "ctx", 1).astype(f32)
    from_after = passed_along(extended[:, :OV].astype(bf16), "ctx", -1).astype(f32)
    middle = extended[:, OV : OV + PATCH]
    return jnp.concatenate(
        [
            middle[:, :OV] + from_before,
            middle[:, OV : PATCH - OV],
            middle[:, PATCH - OV :] + from_after,
        ],
        axis=1,
    )


def body(tokens, w_qkv, w_out, w_dec):
    fits = lax.axis_size("ctx") == 8 and lax.axis_size("head") == 4
    fits = fits and w_qkv.shape[2] == 4 * LANES and tokens.shape[0] % 256 == 0
    run = fast_body if fits else general_body
    return run(tokens, w_qkv, w_out, w_dec)


def solution(mesh):
    return jax.shard_map(
        body,
        mesh=mesh,
        in_specs=(P("ctx", None), P(None, None, "head"), P("head", None), P(None, None, "head")),
        out_specs=P("ctx", None, "head"),
        check_vma=False,
    )
```

```python
import functools
import math

import jax
import jax.numpy as jnp
from jax import lax
from jax.experimental import pallas as pl
from jax.experimental.pallas import tpu as pltpu
from jax.sharding import PartitionSpec as P

HD = 64
PATCH = 8
OV = 2
LANES = 128

eps = 1e-05
bf16 = jnp.bfloat16
f32 = jnp.float32


def passed_along(value, axis, steps):
    count = lax.axis_size(axis)
    pairs = [(source, (source + steps) % count) for source in range(count)]
    return lax.ppermute(value, axis, pairs)


def swapped(value, axis, bits):
    count = lax.axis_size(axis)
    return lax.ppermute(value, axis, [(i, i ^ bits) for i in range(count)])


def rms_scale(values):
    return values * lax.rsqrt(jnp.mean(values * values, axis=-1, keepdims=True) + eps)


def place():
    ctx = lax.axis_index("ctx")
    return lax.div(ctx, 2), lax.rem(ctx, 2)


def project_kernel(x_hbm, w_hbm, *refs):
    packs = refs[:4]
    x_ref, w_ref, x_sem, w_sem = refs[4:]
    z, _ = place()
    rows = x_ref.shape[0]
    x_copy = pltpu.make_async_copy(x_hbm, x_ref, x_sem)
    x_copy.start()
    copies = [pltpu.make_async_copy(w_hbm.at[k], w_ref.at[k], w_sem.at[k]) for k in range(3)]
    copies[0].start()
    x_copy.wait()
    copies[1].start()
    copies[2].start()
    x = x_ref[...].astype(f32)
    scale = lax.rsqrt(jnp.mean(x * x, axis=-1, keepdims=True) + eps)
    q_scale = scale * (HD ** (-0.5) * math.log2(math.e))
    odd = lax.rem(z, 2) == 1
    upper = lax.div(z, 2) == 1
    for k, copy in enumerate(copies):
        copy.wait()
        out = jnp.dot(x_ref[...], w_ref[k], preferred_element_type=f32)
        out = (out * (q_scale if k == 0 else scale)).astype(bf16)
        parts = [out[:, i * LANES : (i + 1) * LANES] for i in range(4)]
        parts = [jnp.where(odd, parts[i ^ 1], parts[i]) for i in range(4)]
        parts = [jnp.where(upper, parts[i ^ 2], parts[i]) for i in range(4)]
        for pack, part in zip(packs, parts):
            pack[pl.ds(k * rows, rows)] = part


def project(tokens, w_qkv):
    rows, width = tokens.shape
    hbm = pl.BlockSpec(memory_space=pltpu.HBM)
    vmem = pl.BlockSpec(memory_space=pltpu.VMEM)
    return pl.pallas_call(
        project_kernel,
        in_specs=[hbm] * 2,
        out_specs=[vmem] * 4,
        out_shape=[jax.ShapeDtypeStruct((3 * rows, LANES), bf16)] * 4,
        scratch_shapes=[
            pltpu.VMEM((rows, width), bf16),
            pltpu.VMEM(w_qkv.shape, bf16),
            pltpu.SemaphoreType.DMA(()),
            pltpu.SemaphoreType.DMA((3,)),
        ],
        compiler_params=pltpu.CompilerParams(vmem_limit_bytes=53 * 2**20),
        name="project",
    )(tokens, w_qkv)


def attention_kernel(count, *refs):
    queries, packs, outs = refs[:count], refs[count : count + 8], refs[count + 8 :]
    rows = outs[0].shape[0]
    low = lax.broadcasted_iota(jnp.int32, (1, LANES), 1) < HD
    one = jnp.ones((), bf16)
    zero = jnp.zeros((), bf16)
    q = jnp.concatenate([pack[:rows] for pack in queries], axis=0)
    k = jnp.concatenate([pack[rows : 2 * rows] for pack in packs], axis=0)
    v = jnp.concatenate([pack[2 * rows :] for pack in packs], axis=0)

    def score(part):
        return lax.dot_general(part, k, (((1,), (1,)), ((), ())), preferred_element_type=f32)

    def weigh(scores):
        return jnp.exp2(scores - jnp.max(scores, axis=-1, keepdims=True)).astype(bf16)

    lo_scores = score(jnp.where(low, q, zero))
    hi_scores = score(jnp.where(low, zero, q))
    lo_weights, hi_weights = weigh(lo_scores), weigh(hi_scores)
    lo = jnp.dot(lo_weights, jnp.where(low, v, one), preferred_element_type=f32)
    hi = jnp.dot(hi_weights, jnp.where(low, one, v), preferred_element_type=f32)
    top = jnp.where(low, lo, hi)
    bottom = pltpu.roll(jnp.where(low, hi, lo), HD, 1)
    attended = (top / bottom).astype(bf16)
    for i, out in enumerate(outs):
        out[...] = attended[i * rows : (i + 1) * rows]


def attend(queries, packs):
    rows = packs[0].shape[0] // 3
    vmem = pl.BlockSpec(memory_space=pltpu.VMEM)
    count = len(queries)
    return pl.pallas_call(
        functools.partial(attention_kernel, count),
        in_specs=[vmem] * (count + len(packs)),
        out_specs=[vmem] * count,
        out_shape=[jax.ShapeDtypeStruct((rows, LANES), bf16)] * count,
        compiler_params=pltpu.CompilerParams(vmem_limit_bytes=24 * 2**20),
        name="attend",
    )(*queries, *packs)


def mix_kernel(x_ref, o0, o1, o2, own, w1, w2, total, att):
    z, _ = place()
    rows, width = x_ref.shape
    local = own.shape[0]
    for s in range(4):
        for i, o in enumerate((o0, o1, o2)):
            at = pl.multiple_of(i * local + (z ^ s) * LANES, LANES)
            att[:, pl.ds(at, LANES)] = o[pl.ds(s * rows, rows)]
    step = 512
    for n in range(0, width, step):
        w = jnp.concatenate([part[:, n : n + step] for part in (own, w1, w2)], axis=0)
        mixed = jnp.dot(att[...], w, preferred_element_type=f32)
        total[:, n : n + step] = x_ref[:, n : n + step].astype(f32) + mixed


def mix(tokens, outs, parts):
    rows, width = tokens.shape
    vmem = pl.BlockSpec(memory_space=pltpu.VMEM)
    return pl.pallas_call(
        mix_kernel,
        in_specs=[vmem] * 7,
        out_specs=vmem,
        out_shape=jax.ShapeDtypeStruct((rows, width), f32),
        scratch_shapes=[pltpu.VMEM((rows, 3 * parts[0].shape[0]), bf16)],
        compiler_params=pltpu.CompilerParams(vmem_limit_bytes=12 * 2**20),
        name="mix",
    )(tokens, *outs, *parts)


def edges_kernel(total, o3, n3, f3, dec_ref, hidden, inner, outer, att, held):
    z, core = place()
    rows, width = total.shape
    for s in range(4):
        spot = z ^ s ^ (2 * core)
        att[:, pl.ds(pl.multiple_of(spot * LANES, LANES), LANES)] = o3[pl.ds(s * rows, rows)]
    step = 512
    squares = jnp.zeros((rows, LANES), f32)
    for n in range(0, width, step):
        w = jnp.concatenate([part[:, n : n + step] for part in (n3, f3)], axis=0)
        mixed = total[:, n : n + step] + jnp.dot(att[...], w, preferred_element_type=f32)
        held[:, n : n + step] = mixed
        for i in range(0, step, LANES):
            squares += mixed[:, i : i + LANES] * mixed[:, i : i + LANES]
    scale = lax.rsqrt(jnp.sum(squares, axis=-1, keepdims=True) * (1.0 / width) + eps)
    hidden[...] = (held[...] * scale).astype(bf16)
    edge = inner.shape[0]
    last = dec_ref.shape[0] - edge

    def cells(part):
        return lax.dot_general(
            dec_ref[part], hidden[...], (((1,), (1,)), ((), ())), preferred_element_type=f32
        ).astype(bf16)

    down = cells(pl.ds(0, edge))
    up = cells(pl.ds(last, edge))
    inner[...] = jnp.where(core == 0, up, down)
    outer[...] = jnp.where(core == 0, down, up)


def decode_edges(total, o3, n3, f3, w_dec):
    rows, width = total.shape
    cells = w_dec.shape[0] // (PATCH + 2 * OV)
    vmem = pl.BlockSpec(memory_space=pltpu.VMEM)
    edge = jax.ShapeDtypeStruct((OV * cells, rows), bf16)
    return pl.pallas_call(
        edges_kernel,
        in_specs=[vmem] * 5,
        out_specs=[vmem] * 3,
        out_shape=[jax.ShapeDtypeStruct((rows, width), bf16), edge, edge],
        scratch_shapes=[
            pltpu.VMEM((rows, n3.shape[0] + f3.shape[0]), bf16),
            pltpu.VMEM((rows, width), f32),
        ],
        compiler_params=pltpu.CompilerParams(vmem_limit_bytes=12 * 2**20),
        name="decode_edges",
    )(total, o3, n3, f3, w_dec)


def main_kernel(hidden, dec_ref, main):
    edge = (dec_ref.shape[0] - main.shape[0]) // 2
    main[...] = lax.dot_general(
        dec_ref[pl.ds(edge, main.shape[0])],
        hidden[...],
        (((1,), (1,)), ((), ())),
        preferred_element_type=f32,
    )


def decode_main(hidden, w_dec):
    cells = w_dec.shape[0] // (PATCH + 2 * OV)
    vmem = pl.BlockSpec(memory_space=pltpu.VMEM)
    return pl.pallas_call(
        main_kernel,
        in_specs=[vmem] * 2,
        out_specs=vmem,
        out_shape=jax.ShapeDtypeStruct((PATCH * cells, hidden.shape[0]), f32),
        compiler_params=pltpu.CompilerParams(vmem_limit_bytes=8 * 2**20),
        name="decode_main",
    )(hidden, w_dec)


def join_kernel(main, inner, outer, field):
    _, core = place()
    edge = inner.shape[0]
    rest = main.shape[0] - edge
    before = jnp.where(core == 0, outer[...], inner[...]).astype(f32)
    after = jnp.where(core == 0, inner[...], outer[...]).astype(f32)
    field[:edge] = main[:edge] + before
    field[edge:rest] = main[edge:rest]
    field[rest:] = main[rest:] + after


def join(main, inner, outer):
    vmem = pl.BlockSpec(memory_space=pltpu.VMEM)
    return pl.pallas_call(
        join_kernel,
        in_specs=[vmem] * 3,
        out_specs=vmem,
        out_shape=jax.ShapeDtypeStruct(main.shape, f32),
        compiler_params=pltpu.CompilerParams(vmem_limit_bytes=4 * 2**20),
        name="join",
    )(main, inner, outer)


def gathered_kernel(*refs):
    rows = refs[0].shape[0]
    for i, part in enumerate(refs[:-1]):
        refs[-1][pl.ds(i * rows, rows)] = part[...]


def gathered(parts):
    rows, width = parts[0].shape
    vmem = pl.BlockSpec(memory_space=pltpu.VMEM)
    return pl.pallas_call(
        gathered_kernel,
        in_specs=[vmem] * len(parts),
        out_specs=vmem,
        out_shape=jax.ShapeDtypeStruct((len(parts) * rows, width), bf16),
        compiler_params=pltpu.CompilerParams(vmem_limit_bytes=4 * 2**20),
        name="gathered",
    )(*parts)


def halved_kernel(block, half):
    _, core = place()
    rows = half.shape[0]
    half[...] = block[pl.ds(pl.multiple_of(core * rows, rows), rows)]


def halved(block):
    rows, width = block.shape
    vmem = pl.BlockSpec(memory_space=pltpu.VMEM)
    return pl.pallas_call(
        halved_kernel,
        in_specs=[vmem],
        out_specs=vmem,
        out_shape=jax.ShapeDtypeStruct((rows // 2, width), bf16),
        compiler_params=pltpu.CompilerParams(vmem_limit_bytes=4 * 2**20),
        name="halved",
    )(block)


def first_way(value):
    count = lax.axis_size("ctx") * lax.axis_size("head")
    pairs = [(i, i ^ (1 if (i // 4) % 2 == 0 else 2)) for i in range(count)]
    return lax.ppermute(value, ("ctx", "head"), pairs)


def second_way(value):
    count = lax.axis_size("ctx") * lax.axis_size("head")
    pairs = [(i, i ^ (2 if (i // 4) % 2 == 0 else 1)) for i in range(count)]
    return lax.ppermute(value, ("ctx", "head"), pairs)


def fast_body(tokens, w_qkv, w_out, w_dec):
    rows = tokens.shape[0]

    w1 = first_way(w_out)

    p0, p1, p2, p3 = project(tokens, w_qkv)
    r2, r3 = swapped(p2, "ctx", 4), swapped(p3, "ctx", 6)
    c0 = swapped(p0, "ctx", 1)
    p1, c0 = lax.optimization_barrier((p1, c0))
    r1 = swapped(p1, "ctx", 2)
    c1, c2, c3 = (swapped(part, "ctx", 1) for part in (r1, r2, r3))
    w1, c1, c2, c3 = lax.optimization_barrier((w1, c1, c2, c3))
    n3 = second_way(halved(w1))

    packs = [p0, r1, r2, r3, c0, c1, c2, c3]
    o2, o3 = attend([r2, r3], packs)
    w1, o2, o3 = lax.optimization_barrier((w1, o2, o3))
    w2 = swapped(w1, "ctx", 1)
    (o1,) = attend([r1], packs)
    p0, o1 = lax.optimization_barrier((p0, o1))
    (o0,) = attend([p0], packs)
    own = gathered([o0, swapped(o1, "ctx", 2), swapped(o2, "ctx", 4), swapped(o3, "ctx", 6)])
    own, n3 = lax.optimization_barrier((own, n3))
    a1, a2 = first_way(own), second_way(own)
    a1, a2, n3 = lax.optimization_barrier((a1, a2, n3))
    a3 = second_way(a1)
    f3 = swapped(n3, "ctx", 1)
    total = mix(tokens, [own, a1, a2], [w_out, w1, w2])

    dec = w_dec.transpose(1, 2, 0)
    dec = dec.reshape(-1, dec.shape[2])
    hidden, inner, outer = decode_edges(total, a3, n3, f3, dec)
    count = lax.axis_size("ctx")
    pairs = [(i, (i - 1 + 2 * (i % 2)) % count) for i in range(count)]
    outer = lax.ppermute(outer, "ctx", pairs)
    inner = swapped(inner, "ctx", 1)
    field = join(decode_main(hidden, dec), inner, outer)
    return field.reshape(PATCH, -1, rows).transpose(2, 0, 1)


def general_body(tokens, w_qkv, w_out, w_dec):
    rows = tokens.shape[0]
    local_heads = w_qkv.shape[2] // HD
    xf = tokens.astype(f32)
    normed = rms_scale(xf).astype(bf16)
    projected = jnp.einsum("td,kdc->ktc", normed, w_qkv, preferred_element_type=f32).astype(bf16)
    queries = projected[0].reshape(rows, local_heads, HD)
    keyvals = projected[1:]
    scale = HD ** (-0.5)

    def block_update(carry, block):
        best, total, accum = carry
        keys = block[0].reshape(-1, local_heads, HD)
        values = block[1].reshape(-1, local_heads, HD)
        scores = jnp.einsum("thd,rhd->thr", queries, keys, preferred_element_type=f32) * scale
        fresh = jnp.maximum(best, jnp.max(scores, axis=-1))
        shrink = jnp.exp(best - fresh)
        weights = jnp.exp(scores - fresh[..., None])
        total = total * shrink + jnp.sum(weights, axis=-1)
        accum = accum * shrink[..., None] + jnp.einsum(
            "thr,rhd->thd", weights.astype(bf16), values, preferred_element_type=f32
        )
        return (fresh, total, accum)

    initial = (
        jnp.full((rows, local_heads), -1e30, f32),
        jnp.zeros((rows, local_heads), f32),
        jnp.zeros((rows, local_heads, HD), f32),
    )
    piece = lax.all_gather(keyvals, "ctx", axis=1, tiled=True)
    length = piece.shape[1]
    span = math.gcd(length, 1024)

    def one_block(index, inner):
        block = lax.dynamic_slice_in_dim(piece, index * span, span, 1)
        return block_update(inner, block)

    best, total, accum = lax.fori_loop(0, length // span, one_block, initial)
    attended = (accum / total[..., None]).astype(bf16).reshape(rows, local_heads * HD)
    partial_out = jnp.dot(attended, w_out, preferred_element_type=f32)
    mixed = lax.psum(partial_out.astype(bf16), "head").astype(f32)
    hidden = rms_scale(xf + mixed).astype(bf16)
    extended = jnp.dot(hidden, w_dec.reshape(w_dec.shape[0], -1), preferred_element_type=f32)
    extended = extended.reshape(rows, w_dec.shape[1], w_dec.shape[2])
    from_before = passed_along(extended[:, PATCH + OV :].astype(bf16), "ctx", 1).astype(f32)
    from_after = passed_along(extended[:, :OV].astype(bf16), "ctx", -1).astype(f32)
    middle = extended[:, OV : OV + PATCH]
    return jnp.concatenate(
        [
            middle[:, :OV] + from_before,
            middle[:, OV : PATCH - OV],
            middle[:, PATCH - OV :] + from_after,
        ],
        axis=1,
    )


def body(tokens, w_qkv, w_out, w_dec):
    fits = lax.axis_size("ctx") == 8 and lax.axis_size("head") == 4
    fits = fits and w_qkv.shape[2] == 4 * LANES and tokens.shape[0] % 256 == 0
    run = fast_body if fits else general_body
    return run(tokens, w_qkv, w_out, w_dec)


def solution(mesh):
    return jax.shard_map(
        body,
        mesh=mesh,
        in_specs=(P("ctx", None), P(None, None, "head"), P("head", None), P(None, None, "head")),
        out_specs=P("ctx", None, "head"),
        check_vma=False,
    )
```

```python
import functools
import math

import jax
import jax.numpy as jnp
from jax import lax
from jax.experimental import pallas as pl
from jax.experimental.pallas import tpu as pltpu
from jax.sharding import PartitionSpec as P

HD = 64
PATCH = 8
OV = 2
LANES = 128

eps = 1e-05
bf16 = jnp.bfloat16
f32 = jnp.float32


def passed_along(value, axis, steps):
    count = lax.axis_size(axis)
    pairs = [(source, (source + steps) % count) for source in range(count)]
    return lax.ppermute(value, axis, pairs)


def swapped(value, axis, bits):
    count = lax.axis_size(axis)
    return lax.ppermute(value, axis, [(i, i ^ bits) for i in range(count)])


def rms_scale(values):
    return values * lax.rsqrt(jnp.mean(values * values, axis=-1, keepdims=True) + eps)


def place():
    ctx = lax.axis_index("ctx")
    return lax.div(ctx, 2), lax.rem(ctx, 2)


def project_kernel(x_hbm, w_hbm, *refs):
    packs = refs[:4]
    x_ref, w_ref, x_sem, w_sem = refs[4:]
    z, _ = place()
    rows = x_ref.shape[0]
    x_copy = pltpu.make_async_copy(x_hbm, x_ref, x_sem)
    x_copy.start()
    copies = [pltpu.make_async_copy(w_hbm.at[k], w_ref.at[k], w_sem.at[k]) for k in range(3)]
    copies[0].start()
    x_copy.wait()
    copies[1].start()
    copies[2].start()
    x = x_ref[...].astype(f32)
    scale = lax.rsqrt(jnp.mean(x * x, axis=-1, keepdims=True) + eps)
    q_scale = scale * (HD ** (-0.5) * math.log2(math.e))
    odd = lax.rem(z, 2) == 1
    upper = lax.div(z, 2) == 1
    for k, copy in enumerate(copies):
        copy.wait()
        out = jnp.dot(x_ref[...], w_ref[k], preferred_element_type=f32)
        out = (out * (q_scale if k == 0 else scale)).astype(bf16)
        parts = [out[:, i * LANES : (i + 1) * LANES] for i in range(4)]
        parts = [jnp.where(odd, parts[i ^ 1], parts[i]) for i in range(4)]
        parts = [jnp.where(upper, parts[i ^ 2], parts[i]) for i in range(4)]
        for pack, part in zip(packs, parts):
            pack[pl.ds(k * rows, rows)] = part


def project(tokens, w_qkv):
    rows, width = tokens.shape
    hbm = pl.BlockSpec(memory_space=pltpu.HBM)
    vmem = pl.BlockSpec(memory_space=pltpu.VMEM)
    return pl.pallas_call(
        project_kernel,
        in_specs=[hbm] * 2,
        out_specs=[vmem] * 4,
        out_shape=[jax.ShapeDtypeStruct((3 * rows, LANES), bf16)] * 4,
        scratch_shapes=[
            pltpu.VMEM((rows, width), bf16),
            pltpu.VMEM(w_qkv.shape, bf16),
            pltpu.SemaphoreType.DMA(()),
            pltpu.SemaphoreType.DMA((3,)),
        ],
        compiler_params=pltpu.CompilerParams(vmem_limit_bytes=53 * 2**20),
        name="project",
    )(tokens, w_qkv)


def attention_kernel(count, *refs):
    queries, packs, outs = refs[:count], refs[count : count + 8], refs[count + 8 :]
    rows = outs[0].shape[0]
    low = lax.broadcasted_iota(jnp.int32, (1, LANES), 1) < HD
    one = jnp.ones((), bf16)
    zero = jnp.zeros((), bf16)
    q = jnp.concatenate([pack[:rows] for pack in queries], axis=0)
    k = jnp.concatenate([pack[rows : 2 * rows] for pack in packs], axis=0)
    v = jnp.concatenate([pack[2 * rows :] for pack in packs], axis=0)

    def score(part):
        return lax.dot_general(part, k, (((1,), (1,)), ((), ())), preferred_element_type=f32)

    def weigh(scores):
        return jnp.exp2(scores - jnp.max(scores, axis=-1, keepdims=True)).astype(bf16)

    lo_scores = score(jnp.where(low, q, zero))
    hi_scores = score(jnp.where(low, zero, q))
    lo_weights, hi_weights = weigh(lo_scores), weigh(hi_scores)
    lo = jnp.dot(lo_weights, jnp.where(low, v, one), preferred_element_type=f32)
    hi = jnp.dot(hi_weights, jnp.where(low, one, v), preferred_element_type=f32)
    top = jnp.where(low, lo, hi)
    bottom = pltpu.roll(jnp.where(low, hi, lo), HD, 1)
    attended = (top / bottom).astype(bf16)
    for i, out in enumerate(outs):
        out[...] = attended[i * rows : (i + 1) * rows]


def attend(queries, packs):
    rows = packs[0].shape[0] // 3
    vmem = pl.BlockSpec(memory_space=pltpu.VMEM)
    count = len(queries)
    return pl.pallas_call(
        functools.partial(attention_kernel, count),
        in_specs=[vmem] * (count + len(packs)),
        out_specs=[vmem] * count,
        out_shape=[jax.ShapeDtypeStruct((rows, LANES), bf16)] * count,
        compiler_params=pltpu.CompilerParams(vmem_limit_bytes=24 * 2**20),
        name="attend",
    )(*queries, *packs)


def mix_kernel(x_ref, o0, o1, o2, own, w1, w2, total, att):
    z, _ = place()
    rows, width = x_ref.shape
    local = own.shape[0]
    for s in range(4):
        for i, o in enumerate((o0, o1, o2)):
            at = pl.multiple_of(i * local + (z ^ s) * LANES, LANES)
            att[:, pl.ds(at, LANES)] = o[pl.ds(s * rows, rows)]
    step = 512
    for n in range(0, width, step):
        w = jnp.concatenate([part[:, n : n + step] for part in (own, w1, w2)], axis=0)
        mixed = jnp.dot(att[...], w, preferred_element_type=f32)
        total[:, n : n + step] = x_ref[:, n : n + step].astype(f32) + mixed


def mix(tokens, outs, parts):
    rows, width = tokens.shape
    vmem = pl.BlockSpec(memory_space=pltpu.VMEM)
    return pl.pallas_call(
        mix_kernel,
        in_specs=[vmem] * 7,
        out_specs=vmem,
        out_shape=jax.ShapeDtypeStruct((rows, width), f32),
        scratch_shapes=[pltpu.VMEM((rows, 3 * parts[0].shape[0]), bf16)],
        compiler_params=pltpu.CompilerParams(vmem_limit_bytes=12 * 2**20),
        name="mix",
    )(tokens, *outs, *parts)


def edges_kernel(total, o3, n3, f3, dec_ref, hidden, scale, inner, outer, att):
    z, core = place()
    rows, width = total.shape
    for s in range(4):
        spot = z ^ s ^ (2 * core)
        att[:, pl.ds(pl.multiple_of(spot * LANES, LANES), LANES)] = o3[pl.ds(s * rows, rows)]
    step = 512
    squares = jnp.zeros((rows, LANES), f32)
    for n in range(0, width, step):
        w = jnp.concatenate([part[:, n : n + step] for part in (n3, f3)], axis=0)
        mixed = total[:, n : n + step] + jnp.dot(att[...], w, preferred_element_type=f32)
        hidden[:, n : n + step] = mixed.astype(bf16)
        for i in range(0, step, LANES):
            squares += mixed[:, i : i + LANES] * mixed[:, i : i + LANES]
    mean = jnp.sum(squares.T, axis=0, keepdims=True) * (1.0 / width)
    factor = lax.rsqrt(mean + eps)
    scale[...] = jnp.broadcast_to(factor, scale.shape)
    edge = inner.shape[0]
    last = dec_ref.shape[0] - edge

    def cells(part):
        out = lax.dot_general(
            dec_ref[part], hidden[...], (((1,), (1,)), ((), ())), preferred_element_type=f32
        )
        return (out * factor).astype(bf16)

    down = cells(pl.ds(0, edge))
    up = cells(pl.ds(last, edge))
    inner[...] = jnp.where(core == 0, up, down)
    outer[...] = jnp.where(core == 0, down, up)


def decode_edges(total, o3, n3, f3, w_dec):
    rows, width = total.shape
    cells = w_dec.shape[0] // (PATCH + 2 * OV)
    vmem = pl.BlockSpec(memory_space=pltpu.VMEM)
    edge = jax.ShapeDtypeStruct((OV * cells, rows), bf16)
    return pl.pallas_call(
        edges_kernel,
        in_specs=[vmem] * 5,
        out_specs=[vmem] * 4,
        out_shape=[
            jax.ShapeDtypeStruct((rows, width), bf16),
            jax.ShapeDtypeStruct((8, rows), f32),
            edge,
            edge,
        ],
        scratch_shapes=[pltpu.VMEM((rows, n3.shape[0] + f3.shape[0]), bf16)],
        compiler_params=pltpu.CompilerParams(vmem_limit_bytes=12 * 2**20),
        name="decode_edges",
    )(total, o3, n3, f3, w_dec)


def main_kernel(hidden, scale, dec_ref, field, ends, main, sem):
    cells = main.shape[0]
    edge = (dec_ref.shape[0] - cells) // 2
    main[...] = scale[:1] * lax.dot_general(
        dec_ref[pl.ds(edge, cells)],
        hidden[...],
        (((1,), (1,)), ((), ())),
        preferred_element_type=f32,
    )
    middle = pl.ds(edge, cells - 2 * edge)
    copy = pltpu.make_async_copy(main.at[middle], field.at[middle], sem)
    copy.start()
    ends[:edge] = main[:edge]
    ends[edge:] = main[cells - edge :]
    copy.wait()


def decode_main(hidden, scale, w_dec):
    rows = hidden.shape[0]
    cells = w_dec.shape[0] // (PATCH + 2 * OV)
    vmem = pl.BlockSpec(memory_space=pltpu.VMEM)
    return pl.pallas_call(
        main_kernel,
        in_specs=[vmem] * 3,
        out_specs=[pl.BlockSpec(memory_space=pltpu.HBM), vmem],
        out_shape=[
            jax.ShapeDtypeStruct((PATCH * cells, rows), f32),
            jax.ShapeDtypeStruct((2 * OV * cells, rows), f32),
        ],
        scratch_shapes=[
            pltpu.VMEM((PATCH * cells, rows), f32),
            pltpu.SemaphoreType.DMA(()),
        ],
        compiler_params=pltpu.CompilerParams(vmem_limit_bytes=8 * 2**20),
        name="decode_main",
    )(hidden, scale, w_dec)


def join_kernel(middle, ends, inner, outer, field, before, after, sems):
    del middle
    _, core = place()
    edge = inner.shape[0]
    last = field.shape[0] - edge
    before[...] = ends[:edge] + jnp.where(core == 0, outer[...], inner[...]).astype(f32)
    first = pltpu.make_async_copy(before, field.at[pl.ds(0, edge)], sems.at[0])
    first.start()
    after[...] = ends[edge:] + jnp.where(core == 0, inner[...], outer[...]).astype(f32)
    second = pltpu.make_async_copy(after, field.at[pl.ds(last, edge)], sems.at[1])
    second.start()
    first.wait()
    second.wait()


def join(field, ends, inner, outer):
    hbm = pl.BlockSpec(memory_space=pltpu.HBM)
    vmem = pl.BlockSpec(memory_space=pltpu.VMEM)
    part = pltpu.VMEM(inner.shape, f32)
    return pl.pallas_call(
        join_kernel,
        in_specs=[hbm, vmem, vmem, vmem],
        out_specs=hbm,
        out_shape=jax.ShapeDtypeStruct(field.shape, f32),
        scratch_shapes=[part, part, pltpu.SemaphoreType.DMA((2,))],
        input_output_aliases={0: 0},
        compiler_params=pltpu.CompilerParams(vmem_limit_bytes=4 * 2**20),
        name="join",
    )(field, ends, inner, outer)


def gathered_kernel(*refs):
    rows = refs[0].shape[0]
    for i, part in enumerate(refs[:-1]):
        refs[-1][pl.ds(i * rows, rows)] = part[...]


def gathered(parts):
    rows, width = parts[0].shape
    vmem = pl.BlockSpec(memory_space=pltpu.VMEM)
    return pl.pallas_call(
        gathered_kernel,
        in_specs=[vmem] * len(parts),
        out_specs=vmem,
        out_shape=jax.ShapeDtypeStruct((len(parts) * rows, width), bf16),
        compiler_params=pltpu.CompilerParams(vmem_limit_bytes=4 * 2**20),
        name="gathered",
    )(*parts)


def halved_kernel(block, half):
    _, core = place()
    rows = half.shape[0]
    half[...] = block[pl.ds(pl.multiple_of(core * rows, rows), rows)]


def halved(block):
    rows, width = block.shape
    vmem = pl.BlockSpec(memory_space=pltpu.VMEM)
    return pl.pallas_call(
        halved_kernel,
        in_specs=[vmem],
        out_specs=vmem,
        out_shape=jax.ShapeDtypeStruct((rows // 2, width), bf16),
        compiler_params=pltpu.CompilerParams(vmem_limit_bytes=4 * 2**20),
        name="halved",
    )(block)


def first_way(value):
    count = lax.axis_size("ctx") * lax.axis_size("head")
    pairs = [(i, i ^ (1 if (i // 4) % 2 == 0 else 2)) for i in range(count)]
    return lax.ppermute(value, ("ctx", "head"), pairs)


def second_way(value):
    count = lax.axis_size("ctx") * lax.axis_size("head")
    pairs = [(i, i ^ (2 if (i // 4) % 2 == 0 else 1)) for i in range(count)]
    return lax.ppermute(value, ("ctx", "head"), pairs)


def fast_body(tokens, w_qkv, w_out, w_dec):
    rows = tokens.shape[0]

    w1 = first_way(w_out)

    p0, p1, p2, p3 = project(tokens, w_qkv)
    r2, r3 = swapped(p2, "ctx", 4), swapped(p3, "ctx", 6)
    c0 = swapped(p0, "ctx", 1)
    p1, c0 = lax.optimization_barrier((p1, c0))
    r1 = swapped(p1, "ctx", 2)
    c1, c2, c3 = (swapped(part, "ctx", 1) for part in (r1, r2, r3))
    w1, c1, c2, c3 = lax.optimization_barrier((w1, c1, c2, c3))
    n3 = second_way(halved(w1))

    packs = [p0, r1, r2, r3, c0, c1, c2, c3]
    o2, o3 = attend([r2, r3], packs)
    w1, o2, o3 = lax.optimization_barrier((w1, o2, o3))
    w2 = swapped(w1, "ctx", 1)
    (o1,) = attend([r1], packs)
    p0, o1 = lax.optimization_barrier((p0, o1))
    (o0,) = attend([p0], packs)
    own = gathered([o0, swapped(o1, "ctx", 2), swapped(o2, "ctx", 4), swapped(o3, "ctx", 6)])
    a1, a2 = first_way(own), second_way(own)
    a1, a2, n3 = lax.optimization_barrier((a1, a2, n3))
    a3 = second_way(a1)
    f3 = swapped(n3, "ctx", 1)
    total = mix(tokens, [own, a1, a2], [w_out, w1, w2])

    dec = w_dec.transpose(1, 2, 0)
    dec = dec.reshape(-1, dec.shape[2])
    hidden, scale, inner, outer = decode_edges(total, a3, n3, f3, dec)
    count = lax.axis_size("ctx")
    pairs = [(i, (i - 1 + 2 * (i % 2)) % count) for i in range(count)]
    outer = lax.ppermute(outer, "ctx", pairs)
    inner = swapped(inner, "ctx", 1)
    field, ends = decode_main(hidden, scale, dec)
    field = join(field, ends, inner, outer)
    return field.reshape(PATCH, -1, rows).transpose(2, 0, 1)


def general_body(tokens, w_qkv, w_out, w_dec):
    rows = tokens.shape[0]
    local_heads = w_qkv.shape[2] // HD
    xf = tokens.astype(f32)
    normed = rms_scale(xf).astype(bf16)
    projected = jnp.einsum("td,kdc->ktc", normed, w_qkv, preferred_element_type=f32).astype(bf16)
    queries = projected[0].reshape(rows, local_heads, HD)
    keyvals = projected[1:]
    scale = HD ** (-0.5)

    def block_update(carry, block):
        best, total, accum = carry
        keys = block[0].reshape(-1, local_heads, HD)
        values = block[1].reshape(-1, local_heads, HD)
        scores = jnp.einsum("thd,rhd->thr", queries, keys, preferred_element_type=f32) * scale
        fresh = jnp.maximum(best, jnp.max(scores, axis=-1))
        shrink = jnp.exp(best - fresh)
        weights = jnp.exp(scores - fresh[..., None])
        total = total * shrink + jnp.sum(weights, axis=-1)
        accum = accum * shrink[..., None] + jnp.einsum(
            "thr,rhd->thd", weights.astype(bf16), values, preferred_element_type=f32
        )
        return (fresh, total, accum)

    initial = (
        jnp.full((rows, local_heads), -1e30, f32),
        jnp.zeros((rows, local_heads), f32),
        jnp.zeros((rows, local_heads, HD), f32),
    )
    piece = lax.all_gather(keyvals, "ctx", axis=1, tiled=True)
    length = piece.shape[1]
    span = math.gcd(length, 1024)

    def one_block(index, inner):
        block = lax.dynamic_slice_in_dim(piece, index * span, span, 1)
        return block_update(inner, block)

    best, total, accum = lax.fori_loop(0, length // span, one_block, initial)
    attended = (accum / total[..., None]).astype(bf16).reshape(rows, local_heads * HD)
    partial_out = jnp.dot(attended, w_out, preferred_element_type=f32)
    mixed = lax.psum(partial_out.astype(bf16), "head").astype(f32)
    hidden = rms_scale(xf + mixed).astype(bf16)
    extended = jnp.dot(hidden, w_dec.reshape(w_dec.shape[0], -1), preferred_element_type=f32)
    extended = extended.reshape(rows, w_dec.shape[1], w_dec.shape[2])
    from_before = passed_along(extended[:, PATCH + OV :].astype(bf16), "ctx", 1).astype(f32)
    from_after = passed_along(extended[:, :OV].astype(bf16), "ctx", -1).astype(f32)
    middle = extended[:, OV : OV + PATCH]
    return jnp.concatenate(
        [
            middle[:, :OV] + from_before,
            middle[:, OV : PATCH - OV],
            middle[:, PATCH - OV :] + from_after,
        ],
        axis=1,
    )


def body(tokens, w_qkv, w_out, w_dec):
    fits = lax.axis_size("ctx") == 8 and lax.axis_size("head") == 4
    fits = fits and w_qkv.shape[2] == 4 * LANES and tokens.shape[0] % 256 == 0
    run = fast_body if fits else general_body
    return run(tokens, w_qkv, w_out, w_dec)


def solution(mesh):
    return jax.shard_map(
        body,
        mesh=mesh,
        in_specs=(P("ctx", None), P(None, None, "head"), P("head", None), P(None, None, "head")),
        out_specs=P("ctx", None, "head"),
        check_vma=False,
    )
```

```python
import functools
import math

import jax
import jax.numpy as jnp
from jax import lax
from jax.experimental import pallas as pl
from jax.experimental.pallas import tpu as pltpu
from jax.sharding import PartitionSpec as P

HD = 64
PATCH = 8
OV = 2
LANES = 128

eps = 1e-05
bf16 = jnp.bfloat16
f32 = jnp.float32


def passed_along(value, axis, steps):
    count = lax.axis_size(axis)
    pairs = [(source, (source + steps) % count) for source in range(count)]
    return lax.ppermute(value, axis, pairs)


def swapped(value, axis, bits):
    count = lax.axis_size(axis)
    return lax.ppermute(value, axis, [(i, i ^ bits) for i in range(count)])


def rms_scale(values):
    return values * lax.rsqrt(jnp.mean(values * values, axis=-1, keepdims=True) + eps)


def place():
    ctx = lax.axis_index("ctx")
    return lax.div(ctx, 2), lax.rem(ctx, 2)


def project_kernel(x_hbm, w_hbm, *refs):
    packs = refs[:4]
    x_ref, w_ref, x_sem, w_sem = refs[4:]
    z, _ = place()
    rows = x_ref.shape[0]
    x_copy = pltpu.make_async_copy(x_hbm, x_ref, x_sem)
    x_copy.start()
    copies = [pltpu.make_async_copy(w_hbm.at[k], w_ref.at[k], w_sem.at[k]) for k in range(3)]
    copies[0].start()
    x_copy.wait()
    copies[1].start()
    copies[2].start()
    x = x_ref[...].astype(f32)
    scale = lax.rsqrt(jnp.mean(x * x, axis=-1, keepdims=True) + eps)
    q_scale = scale * (HD ** (-0.5) * math.log2(math.e))
    odd = lax.rem(z, 2) == 1
    upper = lax.div(z, 2) == 1
    for k, copy in enumerate(copies):
        copy.wait()
        out = jnp.dot(x_ref[...], w_ref[k], preferred_element_type=f32)
        out = (out * (q_scale if k == 0 else scale)).astype(bf16)
        parts = [out[:, i * LANES : (i + 1) * LANES] for i in range(4)]
        parts = [jnp.where(odd, parts[i ^ 1], parts[i]) for i in range(4)]
        parts = [jnp.where(upper, parts[i ^ 2], parts[i]) for i in range(4)]
        for pack, part in zip(packs, parts):
            pack[pl.ds(k * rows, rows)] = part


def project(tokens, w_qkv):
    rows, width = tokens.shape
    hbm = pl.BlockSpec(memory_space=pltpu.HBM)
    vmem = pl.BlockSpec(memory_space=pltpu.VMEM)
    return pl.pallas_call(
        project_kernel,
        in_specs=[hbm] * 2,
        out_specs=[vmem] * 4,
        out_shape=[jax.ShapeDtypeStruct((3 * rows, LANES), bf16)] * 4,
        scratch_shapes=[
            pltpu.VMEM((rows, width), bf16),
            pltpu.VMEM(w_qkv.shape, bf16),
            pltpu.SemaphoreType.DMA(()),
            pltpu.SemaphoreType.DMA((3,)),
        ],
        compiler_params=pltpu.CompilerParams(vmem_limit_bytes=53 * 2**20),
        name="project",
    )(tokens, w_qkv)


def attention_kernel(count, *refs):
    queries, packs, outs = refs[:count], refs[count : count + 8], refs[count + 8 :]
    rows = outs[0].shape[0]
    low = lax.broadcasted_iota(jnp.int32, (1, LANES), 1) < HD
    one = jnp.ones((), bf16)
    zero = jnp.zeros((), bf16)
    q = jnp.concatenate([pack[:rows] for pack in queries], axis=0)
    k = jnp.concatenate([pack[rows : 2 * rows] for pack in packs], axis=0)
    v = jnp.concatenate([pack[2 * rows :] for pack in packs], axis=0)

    def score(part):
        return lax.dot_general(part, k, (((1,), (1,)), ((), ())), preferred_element_type=f32)

    def weigh(scores):
        return jnp.exp2(scores - jnp.max(scores, axis=-1, keepdims=True)).astype(bf16)

    lo_scores = score(jnp.where(low, q, zero))
    hi_scores = score(jnp.where(low, zero, q))
    lo_weights, hi_weights = weigh(lo_scores), weigh(hi_scores)
    lo = jnp.dot(lo_weights, jnp.where(low, v, one), preferred_element_type=f32)
    hi = jnp.dot(hi_weights, jnp.where(low, one, v), preferred_element_type=f32)
    top = jnp.where(low, lo, hi)
    bottom = pltpu.roll(jnp.where(low, hi, lo), HD, 1)
    attended = (top / bottom).astype(bf16)
    for i, out in enumerate(outs):
        out[...] = attended[i * rows : (i + 1) * rows]


def attend(queries, packs):
    rows = packs[0].shape[0] // 3
    vmem = pl.BlockSpec(memory_space=pltpu.VMEM)
    count = len(queries)
    return pl.pallas_call(
        functools.partial(attention_kernel, count),
        in_specs=[vmem] * (count + len(packs)),
        out_specs=[vmem] * count,
        out_shape=[jax.ShapeDtypeStruct((rows, LANES), bf16)] * count,
        compiler_params=pltpu.CompilerParams(vmem_limit_bytes=24 * 2**20),
        name="attend",
    )(*queries, *packs)


def mix_kernel(x_ref, o0, o1, o2, own, w1, w2, total, att):
    z, _ = place()
    rows, width = x_ref.shape
    local = own.shape[0]
    for s in range(4):
        for i, o in enumerate((o0, o1, o2)):
            at = pl.multiple_of(i * local + (z ^ s) * LANES, LANES)
            att[:, pl.ds(at, LANES)] = o[pl.ds(s * rows, rows)]
    step = 512
    for n in range(0, width, step):
        w = jnp.concatenate([part[:, n : n + step] for part in (own, w1, w2)], axis=0)
        mixed = jnp.dot(att[...], w, preferred_element_type=f32)
        total[:, n : n + step] = x_ref[:, n : n + step].astype(f32) + mixed


def mix(tokens, outs, parts):
    rows, width = tokens.shape
    vmem = pl.BlockSpec(memory_space=pltpu.VMEM)
    return pl.pallas_call(
        mix_kernel,
        in_specs=[vmem] * 7,
        out_specs=vmem,
        out_shape=jax.ShapeDtypeStruct((rows, width), f32),
        scratch_shapes=[pltpu.VMEM((rows, 3 * parts[0].shape[0]), bf16)],
        compiler_params=pltpu.CompilerParams(vmem_limit_bytes=12 * 2**20),
        name="mix",
    )(tokens, *outs, *parts)


def edges_kernel(total, o3, n3, f3, dec_ref, hidden, scale, inner, outer, att):
    z, core = place()
    rows, width = total.shape
    for s in range(4):
        spot = z ^ s ^ (2 * core)
        att[:, pl.ds(pl.multiple_of(spot * LANES, LANES), LANES)] = o3[pl.ds(s * rows, rows)]
    step = 512
    squares = jnp.zeros((rows, LANES), f32)
    for n in range(0, width, step):
        w = jnp.concatenate([part[:, n : n + step] for part in (n3, f3)], axis=0)
        mixed = total[:, n : n + step] + jnp.dot(att[...], w, preferred_element_type=f32)
        hidden[:, n : n + step] = mixed.astype(bf16)
        for i in range(0, step, LANES):
            squares += mixed[:, i : i + LANES] * mixed[:, i : i + LANES]
    mean = jnp.sum(squares.T, axis=0, keepdims=True) * (1.0 / width)
    factor = lax.rsqrt(mean + eps)
    scale[...] = jnp.broadcast_to(factor, scale.shape)
    edge = inner.shape[0]
    last = dec_ref.shape[0] - edge

    def cells(part):
        out = lax.dot_general(
            dec_ref[part], hidden[...], (((1,), (1,)), ((), ())), preferred_element_type=f32
        )
        return (out * factor).astype(bf16)

    down = cells(pl.ds(0, edge))
    up = cells(pl.ds(last, edge))
    inner[...] = jnp.where(core == 0, up, down)
    outer[...] = jnp.where(core == 0, down, up)


def decode_edges(total, o3, n3, f3, w_dec):
    rows, width = total.shape
    cells = w_dec.shape[0] // (PATCH + 2 * OV)
    vmem = pl.BlockSpec(memory_space=pltpu.VMEM)
    edge = jax.ShapeDtypeStruct((OV * cells, rows), bf16)
    return pl.pallas_call(
        edges_kernel,
        in_specs=[vmem] * 5,
        out_specs=[vmem] * 4,
        out_shape=[
            jax.ShapeDtypeStruct((rows, width), bf16),
            jax.ShapeDtypeStruct((8, rows), f32),
            edge,
            edge,
        ],
        scratch_shapes=[pltpu.VMEM((rows, n3.shape[0] + f3.shape[0]), bf16)],
        compiler_params=pltpu.CompilerParams(vmem_limit_bytes=12 * 2**20),
        name="decode_edges",
    )(total, o3, n3, f3, w_dec)


def main_kernel(hidden, scale, dec_ref, field, ends, main, sem):
    cells = main.shape[0]
    edge = (dec_ref.shape[0] - cells) // 2
    main[...] = scale[:1] * lax.dot_general(
        dec_ref[pl.ds(edge, cells)],
        hidden[...],
        (((1,), (1,)), ((), ())),
        preferred_element_type=f32,
    )
    middle = pl.ds(edge, cells - 2 * edge)
    copy = pltpu.make_async_copy(main.at[middle], field.at[middle], sem)
    copy.start()
    ends[:edge] = main[:edge]
    ends[edge:] = main[cells - edge :]
    copy.wait()


def decode_main(hidden, scale, w_dec):
    rows = hidden.shape[0]
    cells = w_dec.shape[0] // (PATCH + 2 * OV)
    vmem = pl.BlockSpec(memory_space=pltpu.VMEM)
    return pl.pallas_call(
        main_kernel,
        in_specs=[vmem] * 3,
        out_specs=[pl.BlockSpec(memory_space=pltpu.HBM), vmem],
        out_shape=[
            jax.ShapeDtypeStruct((PATCH * cells, rows), f32),
            jax.ShapeDtypeStruct((2 * OV * cells, rows), f32),
        ],
        scratch_shapes=[
            pltpu.VMEM((PATCH * cells, rows), f32),
            pltpu.SemaphoreType.DMA(()),
        ],
        compiler_params=pltpu.CompilerParams(vmem_limit_bytes=8 * 2**20),
        name="decode_main",
    )(hidden, scale, w_dec)


def join_kernel(middle, ends, inner, outer, field, before, after, sems):
    del middle
    _, core = place()
    edge = inner.shape[0]
    last = field.shape[0] - edge
    before[...] = ends[:edge] + jnp.where(core == 0, outer[...], inner[...]).astype(f32)
    first = pltpu.make_async_copy(before, field.at[pl.ds(0, edge)], sems.at[0])
    first.start()
    after[...] = ends[edge:] + jnp.where(core == 0, inner[...], outer[...]).astype(f32)
    second = pltpu.make_async_copy(after, field.at[pl.ds(last, edge)], sems.at[1])
    second.start()
    first.wait()
    second.wait()


def join(field, ends, inner, outer):
    hbm = pl.BlockSpec(memory_space=pltpu.HBM)
    vmem = pl.BlockSpec(memory_space=pltpu.VMEM)
    part = pltpu.VMEM(inner.shape, f32)
    return pl.pallas_call(
        join_kernel,
        in_specs=[hbm, vmem, vmem, vmem],
        out_specs=hbm,
        out_shape=jax.ShapeDtypeStruct(field.shape, f32),
        scratch_shapes=[part, part, pltpu.SemaphoreType.DMA((2,))],
        input_output_aliases={0: 0},
        compiler_params=pltpu.CompilerParams(vmem_limit_bytes=4 * 2**20),
        name="join",
    )(field, ends, inner, outer)


def gathered_kernel(*refs):
    rows = refs[0].shape[0]
    for i, part in enumerate(refs[:-1]):
        refs[-1][pl.ds(i * rows, rows)] = part[...]


def gathered(parts):
    rows, width = parts[0].shape
    vmem = pl.BlockSpec(memory_space=pltpu.VMEM)
    return pl.pallas_call(
        gathered_kernel,
        in_specs=[vmem] * len(parts),
        out_specs=vmem,
        out_shape=jax.ShapeDtypeStruct((len(parts) * rows, width), bf16),
        compiler_params=pltpu.CompilerParams(vmem_limit_bytes=4 * 2**20),
        name="gathered",
    )(*parts)


def halved_kernel(block, half):
    _, core = place()
    rows = half.shape[0]
    half[...] = block[pl.ds(pl.multiple_of(core * rows, rows), rows)]


def halved(block):
    rows, width = block.shape
    vmem = pl.BlockSpec(memory_space=pltpu.VMEM)
    return pl.pallas_call(
        halved_kernel,
        in_specs=[vmem],
        out_specs=vmem,
        out_shape=jax.ShapeDtypeStruct((rows // 2, width), bf16),
        compiler_params=pltpu.CompilerParams(vmem_limit_bytes=4 * 2**20),
        name="halved",
    )(block)


def first_way(value):
    count = lax.axis_size("ctx") * lax.axis_size("head")
    pairs = [(i, i ^ (1 if (i // 4) % 2 == 0 else 2)) for i in range(count)]
    return lax.ppermute(value, ("ctx", "head"), pairs)


def second_way(value):
    count = lax.axis_size("ctx") * lax.axis_size("head")
    pairs = [(i, i ^ (2 if (i // 4) % 2 == 0 else 1)) for i in range(count)]
    return lax.ppermute(value, ("ctx", "head"), pairs)


def fast_body(tokens, w_qkv, w_out, w_dec):
    rows = tokens.shape[0]

    w1 = first_way(w_out)

    p0, p1, p2, p3 = project(tokens, w_qkv)
    r2, r3 = swapped(p2, "ctx", 4), swapped(p3, "ctx", 6)
    c0 = swapped(p0, "ctx", 1)
    p1, c0 = lax.optimization_barrier((p1, c0))
    r1 = swapped(p1, "ctx", 2)
    c1, c2, c3 = (swapped(part, "ctx", 1) for part in (r1, r2, r3))
    w1, c1, c2, c3 = lax.optimization_barrier((w1, c1, c2, c3))
    n3 = second_way(halved(w1))

    packs = [p0, r1, r2, r3, c0, c1, c2, c3]
    o2, o3 = attend([r2, r3], packs)
    w1, o2, o3 = lax.optimization_barrier((w1, o2, o3))
    w2 = swapped(w1, "ctx", 1)
    (o1,) = attend([r1], packs)
    (o0,) = attend([p0], packs)
    own = gathered([o0, swapped(o1, "ctx", 2), swapped(o2, "ctx", 4), swapped(o3, "ctx", 6)])
    a1, a2 = first_way(own), second_way(own)
    a1, a2, n3 = lax.optimization_barrier((a1, a2, n3))
    a3 = second_way(a1)
    f3 = swapped(n3, "ctx", 1)
    total = mix(tokens, [own, a1, a2], [w_out, w1, w2])

    dec = w_dec.transpose(1, 2, 0)
    dec = dec.reshape(-1, dec.shape[2])
    hidden, scale, inner, outer = decode_edges(total, a3, n3, f3, dec)
    count = lax.axis_size("ctx")
    pairs = [(i, (i - 1 + 2 * (i % 2)) % count) for i in range(count)]
    outer = lax.ppermute(outer, "ctx", pairs)
    inner = swapped(inner, "ctx", 1)
    field, ends = decode_main(hidden, scale, dec)
    field = join(field, ends, inner, outer)
    return field.reshape(PATCH, -1, rows).transpose(2, 0, 1)


def general_body(tokens, w_qkv, w_out, w_dec):
    rows = tokens.shape[0]
    local_heads = w_qkv.shape[2] // HD
    xf = tokens.astype(f32)
    normed = rms_scale(xf).astype(bf16)
    projected = jnp.einsum("td,kdc->ktc", normed, w_qkv, preferred_element_type=f32).astype(bf16)
    queries = projected[0].reshape(rows, local_heads, HD)
    keyvals = projected[1:]
    scale = HD ** (-0.5)

    def block_update(carry, block):
        best, total, accum = carry
        keys = block[0].reshape(-1, local_heads, HD)
        values = block[1].reshape(-1, local_heads, HD)
        scores = jnp.einsum("thd,rhd->thr", queries, keys, preferred_element_type=f32) * scale
        fresh = jnp.maximum(best, jnp.max(scores, axis=-1))
        shrink = jnp.exp(best - fresh)
        weights = jnp.exp(scores - fresh[..., None])
        total = total * shrink + jnp.sum(weights, axis=-1)
        accum = accum * shrink[..., None] + jnp.einsum(
            "thr,rhd->thd", weights.astype(bf16), values, preferred_element_type=f32
        )
        return (fresh, total, accum)

    initial = (
        jnp.full((rows, local_heads), -1e30, f32),
        jnp.zeros((rows, local_heads), f32),
        jnp.zeros((rows, local_heads, HD), f32),
    )
    piece = lax.all_gather(keyvals, "ctx", axis=1, tiled=True)
    length = piece.shape[1]
    span = math.gcd(length, 1024)

    def one_block(index, inner):
        block = lax.dynamic_slice_in_dim(piece, index * span, span, 1)
        return block_update(inner, block)

    best, total, accum = lax.fori_loop(0, length // span, one_block, initial)
    attended = (accum / total[..., None]).astype(bf16).reshape(rows, local_heads * HD)
    partial_out = jnp.dot(attended, w_out, preferred_element_type=f32)
    mixed = lax.psum(partial_out.astype(bf16), "head").astype(f32)
    hidden = rms_scale(xf + mixed).astype(bf16)
    extended = jnp.dot(hidden, w_dec.reshape(w_dec.shape[0], -1), preferred_element_type=f32)
    extended = extended.reshape(rows, w_dec.shape[1], w_dec.shape[2])
    from_before = passed_along(extended[:, PATCH + OV :].astype(bf16), "ctx", 1).astype(f32)
    from_after = passed_along(extended[:, :OV].astype(bf16), "ctx", -1).astype(f32)
    middle = extended[:, OV : OV + PATCH]
    return jnp.concatenate(
        [
            middle[:, :OV] + from_before,
            middle[:, OV : PATCH - OV],
            middle[:, PATCH - OV :] + from_after,
        ],
        axis=1,
    )


def body(tokens, w_qkv, w_out, w_dec):
    fits = lax.axis_size("ctx") == 8 and lax.axis_size("head") == 4
    fits = fits and w_qkv.shape[2] == 4 * LANES and tokens.shape[0] % 256 == 0
    run = fast_body if fits else general_body
    return run(tokens, w_qkv, w_out, w_dec)


def solution(mesh):
    return jax.shard_map(
        body,
        mesh=mesh,
        in_specs=(P("ctx", None), P(None, None, "head"), P("head", None), P(None, None, "head")),
        out_specs=P("ctx", None, "head"),
        check_vma=False,
    )
```
